256 devices in a mesh: rep: 32 (over x, z_hi, core), dom: 8 (over z_lo, y).
Axes of the slice: x: 4, y: 4, z: 8 (z_hi: 4, z_lo: 2; z = z_hi * 2 + z_lo), core: 2. Of those that a mesh axis runs over, the one named last changes fastest.
Arguments:
- tokens: bfloat16 [131072, 1792], P(('rep', 'dom')), may hold values from -6 to 6
- routes: int32 [131072, 8], P(('rep', 'dom')), may hold values from 0 to 63, as said below
- gate_codes: int32 [131072, 8], P(('rep', 'dom')), may hold values from 1 to 64
- cotangent: bfloat16 [131072, 1792], P(('rep', 'dom')), may hold values from -48 to 48
- w_gate: bfloat16 [1792, 1280], P('dom'), may hold values from -0.125 to 0.125
- w_up: bfloat16 [1792, 1280], P('dom'), may hold values from -0.125 to 0.125
- w_down: bfloat16 [1792, 1280], P('dom'), may hold values from -0.15625 to 0.15625
Outputs:
- d_tokens: bfloat16 [131072, 1792], P(('rep', 'dom'))
- grad_gate: float32 [1792, 1280], P('dom')
- grad_up: float32 [1792, 1280], P('dom')
- grad_down: float32 [1792, 1280], P('dom')
The draws below stay inside these ranges and needn't reach their ends.
Inputs may be any that keep to these rules, and one draw needn't show every extreme that they name: `routes`: each row names 8 different experts. In each aligned block of 512 rows (the rows of one device) between 48 and 96 rows name expert 0, and in every draw some block has exactly 96 such rows.
All inputs are finite; a program needn't handle non-finite values.
Results may differ from the reference program's by a relative error of at most 0.015.
Values may be sent and summed in bfloat16 or wider, within the bound.
A program may use at most 128 MiB of HBM per device.

```python
import jax
import jax.numpy as jnp
from jax import lax

D = 1792
FF = 1280
EXPERTS = 64
TOPK = 8
TOK_DEV = 512
CAP = 96
TOKENS = 131072


def draw_routes(key, part):
    key = jax.random.fold_in(key, 11)
    key_count, key_full, key_forced, key_rank, key_expert = jax.random.split(key, 5)
    block_count = TOKENS // TOK_DEV
    counts = jax.random.randint(key_count, (block_count,), CAP // 2, CAP + 1)
    filled = jax.random.randint(key_full, (block_count,), 0, 4) == 0
    forced = jax.random.randint(key_forced, (), 0, block_count)
    filled = filled | (jnp.arange(block_count) == forced)
    counts = jnp.where(filled, CAP, counts)
    scores = jax.random.randint(key_rank, (block_count, TOK_DEV), 0, 2 ** 20) * TOK_DEV + jnp.arange(TOK_DEV)
    ranking = jnp.argsort(jnp.argsort(scores, axis=1), axis=1)
    member = (ranking < counts[:, None]).reshape(TOKENS)
    expert_scores = jax.random.randint(key_expert, (TOKENS, EXPERTS), 0, 2 ** 20) * EXPERTS + jnp.arange(EXPERTS)
    expert_scores = expert_scores.at[:, 0].set(jnp.where(member, 2 ** 30, -1))
    top_values, picked_ids = lax.top_k(expert_scores, TOPK)
    return picked_ids.astype(jnp.int32)


def with_ends(array, key, low, high):
    shape = array.shape
    place = [jax.random.randint(jax.random.fold_in(key, axis), (), 0, shape[axis]) for axis in range(len(shape))]
    array = array.at[tuple(place)].set(low)
    longest = shape.index(max(shape))
    place[longest] = (place[longest] + 1) % shape[longest]
    return array.at[tuple(place)].set(high)


def spiked(values, own_key, source, target, shards_of, factor):
    def block_of(position):
        return (jnp.arange(values.shape[position]) // (values.shape[position] // shards_of)).reshape((-1,) + (1,) * (values.ndim - 1 - position))

    first = jax.random.permutation(own_key, shards_of)[block_of(target)]
    second = (block_of(target) + shards_of // 2) % shards_of
    return jnp.where((block_of(source) == first) | (block_of(source) == second), factor * values, values)


def block_scale(rng, shape, shards, smallest, high):
    gain, own = 1.0, jax.random.fold_in(rng, 6)
    for position, blocks in shards:
        steps = jnp.exp(jax.random.uniform(jax.random.fold_in(own, position), (blocks,), jnp.float32, smallest / len(shards), high / len(shards)))
        gain = gain * jnp.repeat(steps, shape[position] // blocks).reshape([-1 if axis == position else 1 for axis in range(len(shape))])
    return gain


def centred(stream_key, dims, deviation, reach, cuts=(), held_as=jnp.bfloat16):
    array = deviation * jax.random.normal(stream_key, dims, jnp.float32)
    if cuts:
        array = array * block_scale(stream_key, dims, cuts, -0.22, 0.18)
    return jnp.clip(array, -reach, reach).astype(held_as)


def gaussian_with(key, shape, width, limit, shards, heavy, kind=jnp.bfloat16):
    result = width * jax.random.normal(key, shape, jnp.float32)
    if shards:
        result = result * block_scale(key, shape, shards, -0.22, 0.18)
    return jnp.clip(spiked(result, jax.random.fold_in(key, 3), *heavy), -limit, limit).astype(kind)


def setup_inputs(seed: int = 0) -> dict:
    key_list = jax.random.split(jax.random.key(seed), 8)
    tokens = centred(key_list[0], (TOKENS, D), 1.0, 6.0, ((0, 256),))
    routes = draw_routes(jax.random.fold_in(key_list[7], 71), 0)
    gate_codes = with_ends(jax.random.randint(key_list[2], (TOKENS, TOPK), 1, 65), jax.random.fold_in(key_list[2], 1), 1, 64).astype(jnp.int32)
    cotangent = gaussian_with(key_list[3], (TOKENS, D), 2.0, 48.0, ((0, 256),), (0, 1, 256, 6.0))
    w_gate = centred(key_list[4], (D, FF), D ** -0.5, 0.125, ((0, 8),))
    w_up = centred(key_list[5], (D, FF), D ** -0.5, 0.125, ((0, 8),))
    w_down = centred(key_list[6], (D, FF), FF ** -0.5, 0.15625, ((0, 8),))
    return dict(tokens=tokens, routes=routes, gate_codes=gate_codes, cotangent=cotangent, w_gate=w_gate, w_up=w_up, w_down=w_down)


def matmul(left, right):
    return jnp.dot(left, right, preferred_element_type=jnp.float32)


def times_transpose_exact(left, right):
    return lax.dot_general(left.astype(jnp.float32), right.astype(jnp.float32), (((1,), (1,)), ((), ())), precision=lax.Precision.HIGHEST, preferred_element_type=jnp.float32)


def transpose_times(left, right):
    return lax.dot_general(left, right, (((0,), (0,)), ((), ())), preferred_element_type=jnp.float32)


def transpose_times_exact(left, right):
    return lax.dot_general(left.astype(jnp.float32), right.astype(jnp.float32), (((0,), (0,)), ((), ())), precision=lax.Precision.HIGHEST, preferred_element_type=jnp.float32)


def pick_rows(tokens, routes, gate_codes, cotangent):
    token_count = tokens.shape[0]
    member = routes == 0
    routed = jnp.any(member, axis=1)
    gate_weight = jnp.sum(jnp.where(member, gate_codes, 0), axis=1).astype(jnp.float32) / 256.0
    chosen = jnp.nonzero(routed, size=CAP, fill_value=token_count)[0].astype(jnp.int32)
    usable = chosen < token_count
    clipped = jnp.minimum(chosen, token_count - 1).astype(jnp.int32)
    picked = jnp.where(usable[:, None], tokens[clipped], jnp.zeros((), jnp.bfloat16))
    weight_rows = jnp.where(usable, gate_weight[clipped], jnp.zeros((), jnp.float32))
    scaled = (weight_rows[:, None] * cotangent[clipped].astype(jnp.float32)).astype(jnp.bfloat16)
    return chosen, picked, scaled


def swiglu_parts(pre_gate, pre_up):
    sigmoid_gate = jax.nn.sigmoid(pre_gate)
    activated = pre_gate * sigmoid_gate
    hidden = (activated * pre_up).astype(jnp.bfloat16)
    return sigmoid_gate, activated, hidden


def swiglu_back(d_hidden, pre_gate, pre_up, sigmoid_gate, activated):
    d_gate = d_hidden * pre_up * sigmoid_gate * (1.0 + pre_gate * (1.0 - sigmoid_gate))
    d_up = d_hidden * activated
    return d_gate, d_up


def reference(tokens, routes, gate_codes, cotangent, w_gate, w_up, w_down):
    block_count = tokens.shape[0] // TOK_DEV

    def block_pass(carry, block):
        block_tokens, block_routes, block_codes, block_cot = block
        chosen, picked, scaled = pick_rows(block_tokens, block_routes, block_codes, block_cot)
        pre_gate = matmul(picked, w_gate)
        pre_up = matmul(picked, w_up)
        sigmoid_gate, activated, hidden = swiglu_parts(pre_gate, pre_up)
        d_hidden = matmul(scaled, w_down)
        d_gate, d_up = swiglu_back(d_hidden, pre_gate, pre_up, sigmoid_gate, activated)
        d_picked = (times_transpose_exact(d_gate, w_gate) + times_transpose_exact(d_up, w_up)).astype(jnp.bfloat16)
        d_block = jnp.zeros(block_tokens.shape, jnp.bfloat16).at[chosen].set(d_picked, mode="drop")
        terms = (transpose_times_exact(picked, d_gate), transpose_times_exact(picked, d_up), transpose_times(scaled, hidden))
        updated = tuple(
            total + lax.optimization_barrier(term.astype(jnp.bfloat16)).astype(jnp.float32)
            for total, term in zip(carry, terms)
        )
        return updated, d_block

    blocks = (
        tokens.reshape(block_count, TOK_DEV, D),
        routes.reshape(block_count, TOK_DEV, TOPK),
        gate_codes.reshape(block_count, TOK_DEV, TOPK),
        cotangent.reshape(block_count, TOK_DEV, D),
    )
    start_sums = (jnp.zeros((D, FF), jnp.float32), jnp.zeros((D, FF), jnp.float32), jnp.zeros((D, FF), jnp.float32))
    totals, d_blocks = lax.scan(block_pass, start_sums, blocks)
    return d_blocks.reshape(tokens.shape[0], D), totals[0], totals[1], totals[2]
```

```python
import jax
import jax.numpy as jnp
from jax import lax
from jax.experimental import pallas as pl
from jax.experimental.pallas import tpu as pltpu
from jax.sharding import PartitionSpec as P

D, FF, CAP, TOK = 1792, 1280, 96, 512
ROWS = 224
MESH = pl.DeviceIdType.MESH
BF, F32 = jnp.bfloat16, jnp.float32
VMEM_LIMIT = 52 * 1024 * 1024

POS = {0: 0, 1: 1, 3: 2, 2: 3}


def coords():
    r, d = lax.axis_index("rep"), lax.axis_index("dom")
    return r // 8, (r // 2) % 4, r % 2, d // 4, d % 4


def dev(x, zh, c, zl, y):
    return (x * 8 + zh * 2 + c, zl * 4 + y)


def dot(a, b, dims=((1,), (0,))):
    return lax.dot_general(a, b, (dims, ((), ())), preferred_element_type=F32)


def iota(shape, axis):
    return lax.broadcasted_iota(jnp.int32, shape, axis)


def pick_kernel(tok, routes, codes, cot, wg, wu, wd, x_out, w_out, sel_out):
    x, _, c, _, _ = coords()
    f = 2 * x + c
    member = routes[...] == 0
    routed = jnp.max(jnp.where(member, 1.0, 0.0), axis=1, keepdims=True)
    code = jnp.sum(jnp.where(member, codes[...], 0), axis=1, keepdims=True).astype(F32)
    below = jnp.where(iota((TOK, TOK), 1) < iota((TOK, TOK), 0), 1.0, 0.0).astype(BF)
    rank = dot(below, jnp.broadcast_to(routed, (TOK, 128)).astype(BF))
    hit = (rank == iota((TOK, 128), 1).astype(F32)) & (routed > 0.0)
    sel = jnp.where(hit, 1.0, 0.0).astype(BF)
    sel_out[...] = sel
    first = ((0,), (0,))
    weight = dot(sel, jnp.broadcast_to(code, (TOK, 128)).astype(BF), first)[:CAP, :1] * (1.0 / 256.0)

    x_out[0] = dot(sel, tok[...], first)[:CAP].astype(BF)
    x_out[1] = (weight * dot(sel, cot[...], first)[:CAP]).astype(BF)

    tile = pl.multiple_of(f * 128, 128)
    last = pl.multiple_of(1024 + (f // 4) * 128, 128)
    rest = jnp.zeros((ROWS, 128), F32)
    src, dst = iota((128, 128), 0), iota((128, 128), 1)
    for part, w in enumerate((wg, wu, wd)):
        w_out[part] = w[:, pl.ds(tile, 128)]
        move = (src - (f % 4) * 32 == dst - part * 32) & (dst // 32 == part)
        rest += dot(w[:, pl.ds(last, 128)], jnp.where(move, 1.0, 0.0).astype(BF))
    w_out[3] = rest.astype(BF)


def greet(partners):
    barrier = pltpu.get_barrier_semaphore()
    for partner in partners:
        pl.semaphore_signal(barrier, inc=1, device_id=partner, device_id_type=MESH)
    pl.semaphore_wait(barrier, len(partners))


def remote(src, dst, send, recv, index, device):
    return pltpu.make_async_remote_copy(
        src_ref=src, dst_ref=dst, send_sem=send.at[index], recv_sem=recv.at[index],
        device_id=device, device_id_type=MESH,
    )


def swiglu_back(g, u, dh):
    sig = 1.0 / (1.0 + jnp.exp(-g))
    act = g * sig
    return dh * u * sig * (1.0 + g * (1.0 - sig)), dh * act, act * u


def expert_rows(lo, hi, xa, wa, grad, dp, first):
    n = (hi - lo) * CAP
    part = lambda i: wa[i].reshape(D, 128)
    picked = xa[0, lo:hi].reshape(n, D)
    scaled = xa[1, lo:hi].reshape(n, D)
    pre = dot(picked, jnp.concatenate([part(0), part(1)], axis=1))
    down = dot(scaled, jnp.concatenate([part(2), part(3)], axis=1))
    rest = dot(picked, part(3))
    lane = iota((n, 128), 1)
    rest = jnp.where(lane < 64, rest, down[:, 128:])
    dg, du, hid = swiglu_back(pre[:, :128], pre[:, 128:], down[:, :128])
    dg_r, du_r, hid_r = swiglu_back(rest, pltpu.roll(rest, 96, 1), pltpu.roll(rest, 64, 1))
    mix = jnp.where(lane < 32, dg_r, pltpu.roll(du_r, 32, 1))
    rest_p = jnp.where(lane < 64, mix, 0.0).astype(BF)
    rest_s = jnp.where((lane >= 64) & (lane < 96), pltpu.roll(hid_r, 64, 1), 0.0).astype(BF)
    up = jnp.concatenate([dg, du], axis=1).astype(BF)
    low = jnp.concatenate([hid.astype(BF), rest_s], axis=1)
    back = jnp.concatenate([up, rest_p], axis=1)

    def columns(k, carry):
        at = pl.multiple_of(k * 256, 256)
        p_k = xa[0, lo:hi, :, pl.ds(at, 256)].reshape(n, 256)
        s_k = xa[1, lo:hi, :, pl.ds(at, 256)].reshape(n, 256)
        gu = dot(p_k, up, ((0,), (0,)))
        hr = dot(s_k, low, ((0,), (0,)))
        rr = dot(p_k, rest_p, ((0,), (0,)))
        terms = (gu[:, :128], gu[:, 128:], hr[:, :128], hr[:, 128:] + rr)
        for i, term in enumerate(terms):
            if first:
                grad[i, pl.ds(at, 256), :] = term
            else:
                grad[i, pl.ds(at, 256), :] += term
        return carry

    lax.fori_loop(0, D // 256, columns, 0)
    for k in range(D // 256):
        flat = jnp.concatenate([wa.at[i].reshape(D, 128)[k * 256:(k + 1) * 256] for i in (0, 1, 3)], axis=1)
        out = dot(back, flat, ((1,), (1,))).astype(BF)
        dp[lo:hi, :, k * 256:(k + 1) * 256] = out.reshape(hi - lo, CAP, 256)


def expert_kernel(x_ref, w_ref, gb, dp, xa, wa, grad, local, ts, tr, ws, wr):
    x, zh, c, zl, y = coords()
    sib = dev(x, zh, 1 - c, zl, y)
    right, left = dev((x + 1) % 4, zh, c, zl, y), dev((x + 3) % 4, zh, c, zl, y)
    north, south = dev(x, zh, c, zl, (y + 1) % 4), dev(x, zh, c, zl, (y + 3) % 4)
    pair = dev(x, zh, c, 1 - zl, y)
    greet([sib, right, left, north, south, pair])

    dom, dom_z = zl * 4 + y, (1 - zl) * 4 + y
    slot = lambda delta, other: 2 * POS[delta] + other

    def tsend(index, src, dst, device):
        return remote(src, dst, ts, tr, index, device)

    def wsend(index, src, dst, device):
        return remote(src, dst, ws, wr, index, device)

    own = (
        pltpu.make_async_copy(x_ref, xa.at[:, 0], local.at[0]),
        pltpu.make_async_copy(w_ref, wa.at[:, dom], local.at[1]),
    )
    p_right = tsend(0, x_ref.at[0], xa.at[0, slot(3, 0)], right)
    s_left = tsend(1, x_ref.at[1], xa.at[1, slot(1, 0)], left)
    s_right = tsend(2, x_ref.at[1], xa.at[1, slot(3, 0)], right)
    p_left = tsend(3, x_ref.at[0], xa.at[0, slot(1, 0)], left)
    x_sib = tsend(4, x_ref, xa.at[:, slot(0, 1)], sib)
    w_pair = wsend(0, w_ref, wa.at[:, dom], pair)
    w_north = wsend(1, w_ref, wa.at[:, dom], north)
    w_south = wsend(2, w_ref, wa.at[:, dom], south)
    for copy in (p_right, s_left, w_pair, w_north, w_south, s_right, p_left, x_sib, *own):
        copy.start()

    w_pair.wait_recv()
    z_north = wsend(3, wa.at[:, dom_z], wa.at[:, dom_z], north)
    z_south = wsend(4, wa.at[:, dom_z], wa.at[:, dom_z], south)
    z_north.start()
    z_south.start()

    def relay(index, base, up):
        if up:
            block = wa.at[0:2, base + (y + 3) % 4]
            copy = wsend(index, block, block, north)
        else:
            block = wa.at[2:4, base + (y + 1) % 4]
            copy = wsend(index, block, block, south)
        copy.start()
        return copy

    w_north.wait_recv()
    o_north = relay(5, zl * 4, True)
    w_south.wait_recv()
    o_south = relay(6, zl * 4, False)

    p_right.wait_recv()
    p_on = tsend(5, xa.at[0, slot(3, 0)], xa.at[0, slot(2, 0)], right)
    p_on.start()
    s_left.wait_recv()
    s_on = tsend(6, xa.at[1, slot(1, 0)], xa.at[1, slot(2, 0)], left)
    s_on.start()

    def share(index, kind, delta):
        copy = tsend(index, xa.at[kind, slot(delta, 0)], xa.at[kind, slot(delta, 1)], sib)
        copy.start()
        return copy

    shared = [share(7, 0, 3), share(8, 1, 1)]
    z_north.wait_recv()
    r_north = relay(7, (1 - zl) * 4, True)
    z_south.wait_recv()
    r_south = relay(8, (1 - zl) * 4, False)
    s_right.wait_recv()
    shared.append(share(9, 1, 3))
    p_left.wait_recv()
    shared.append(share(10, 0, 1))

    for copy in own:
        copy.wait()
    for copy in (o_north, o_south, r_north, r_south):
        copy.wait_recv()
    x_sib.wait_recv()
    for copy in shared:
        copy.wait_recv()
    expert_rows(0, 6, xa, wa, grad, dp, True)

    p_on.wait_recv()
    last = [share(11, 0, 2)]
    s_on.wait_recv()
    last.append(share(12, 1, 2))
    for copy in last:
        copy.wait_recv()
    expert_rows(6, 8, xa, wa, grad, dp, False)
    for d in range(8):
        gb[:, d // 4, d % 4] = grad[:, d * ROWS:(d + 1) * ROWS, :].astype(BF)

    for copy in (p_right, s_left, s_right, p_left, x_sib, p_on, s_on, *shared, *last,
                 w_pair, w_north, w_south, z_north, z_south, o_north, o_south, r_north, r_south):
        copy.wait_send()


def reduce_kernel(gb, dp, fin, dpick, dr, ds, df, ra, rb, ta, tb, low, high, zs, zr, gs, gr, es, er, ns, nr):
    x, zh, c, zl, y = coords()
    z = zh * 2 + zl
    sib = dev(x, zh, 1 - c, zl, y)
    ring = [dev((x + k) % 4, zh, c, zl, y) for k in (1, 2, 3)]
    yn, ys = (y + 1) % 4, (y + 3) % 4
    north, south = dev(x, zh, c, zl, yn), dev(x, zh, c, zl, ys)
    column = [dev(x, ((z + k) % 8) // 2, c, ((z + k) % 8) % 2, y) for k in range(1, 8)]
    greet([sib, north, south] + ring + column)
    up = lambda ref: ref.astype(F32)
    sends = []

    def send(index, src, dst, device, sems):
        copy = remote(src, dst, *sems, index, device)
        copy.start()
        sends.append(copy)
        return copy

    G, E, N = (gs, gr), (es, er), (ns, nr)
    opposite = (y + 2) % 4
    opp_n = send(0, gb.at[0:2, :, opposite], ra, north, G)
    opp_s = send(1, gb.at[2:4, :, opposite], rb, south, G)
    dir_n = send(2, gb.at[2:4, :, yn], low.at[2:4], north, G)
    dir_s = send(3, gb.at[0:2, :, ys], high.at[0:2], south, G)
    d_sib = send(0, dp.at[:, 1], dr, sib, E)

    opp_n.wait_recv()
    ta[...] = (up(ra[...]) + up(gb[0:2, :, yn])).astype(BF)
    add_n = send(4, ta, low.at[0:2], north, G)
    opp_s.wait_recv()
    tb[...] = (up(rb[...]) + up(gb[2:4, :, ys])).astype(BF)
    add_s = send(5, tb, high.at[2:4], south, G)

    d_sib.wait_recv()
    d_ring = []
    for k in (2, 1, 3):
        ds[k - 1] = (up(dr[POS[k]]) + up(dp[POS[k], 0])).astype(BF)
        d_ring.append(send(k, ds.at[k - 1], df.at[k - 1], ring[k - 1], E))

    for copy in (dir_n, dir_s, add_n, add_s):
        copy.wait_recv()
    zs[...] = (up(gb[:, :, y]) + up(low[...]) + up(high[...])).astype(BF)

    z_sum = []
    for k in (4, 3, 5, 2, 6, 1, 7):
        to = (z + k) % 8
        z_sum.append(send(5 + k, zs.at[to // 2, to % 2], zr.at[k - 1], column[k - 1], G))
    for copy in d_ring:
        copy.wait_recv()
    dpick[...] = (up(dr[0]) + up(dp[0, 0]) + up(df[0]) + up(df[1]) + up(df[2])).astype(BF)
    for copy in z_sum:
        copy.wait_recv()
    total = up(zs[zh, zl])
    for k in range(7):
        total += up(zr[k])
    fin[x, c, zh] = total.astype(BF)

    mine = fin.at[x, c, zh]
    over_z = [send(k - 1, mine, mine, dev(x, (zh + k) % 4, c, zl, y), N) for k in (1, 2, 3)]
    over_x = [[send(3 + k - 1, mine, mine, ring[k - 1], N) for k in (1, 2, 3)]]
    for k in (1, 3, 2):
        over_z[k - 1].wait_recv()
        piece = fin.at[x, c, (zh + 4 - k) % 4]
        over_x.append([send(3 + 3 * k + j - 1, piece, piece, ring[j - 1], N) for j in (1, 2, 3)])
    cores = [send(15, fin.at[x, c], fin.at[x, c], sib, N)]
    for j in (1, 3, 2):
        for copies in over_x:
            copies[j - 1].wait_recv()
        block = fin.at[(x + 4 - j) % 4, c]
        cores.append(send(15 + j, block, block, sib, N))
    for copy in cores:
        copy.wait_recv()
    for copy in sends:
        copy.wait_send()


def finish_kernel(fin, dpick, sel, d_tokens, gg, gu, gd):
    rows = jnp.concatenate([dpick[...], jnp.zeros((128 - CAP, D), BF)], axis=0)
    d_tokens[...] = dot(sel[...], rows).astype(BF)
    lane = iota((ROWS, 128), 1)
    rest = [fin[f, 3].astype(F32) for f in range(8)]
    for part, out in enumerate((gg, gu, gd)):
        for f in range(8):
            out[:, f * 128:(f + 1) * 128] = fin[f, part].astype(F32)
        for half in range(2):
            total = jnp.zeros((ROWS, 128), F32)
            for k in range(4):
                shift = ((k - part) * 32) % 128
                tile = rest[4 * half + k]
                tile = pltpu.roll(tile, shift, 1) if shift else tile
                total = jnp.where(lane // 32 == k, tile, total)
            out[:, 1024 + half * 128:1152 + half * 128] = total


def call(kernel, name, ins, outs, scratch=(), collective=None, flops=0):
    extra = {} if collective is None else dict(collective_id=collective, has_side_effects=True)
    return pl.pallas_call(
        kernel,
        name=name,
        out_shape=[jax.ShapeDtypeStruct(shape, dtype) for shape, dtype in outs],
        in_specs=[pl.BlockSpec(memory_space=pltpu.VMEM)] * ins,
        out_specs=[pl.BlockSpec(memory_space=pltpu.VMEM)] * len(outs),
        scratch_shapes=list(scratch),
        cost_estimate=pl.CostEstimate(flops=flops, bytes_accessed=8_000_000, transcendentals=0),
        compiler_params=pltpu.CompilerParams(vmem_limit_bytes=VMEM_LIMIT, **extra),
    )


def body(tokens, routes, gate_codes, cotangent, w_gate, w_up, w_down):
    dma = lambda n: pltpu.SemaphoreType.DMA((n,))
    buf = lambda *shape: pltpu.VMEM(shape, BF)
    x_own, w_own, sel = call(
        pick_kernel, "pick", 7,
        [((2, CAP, D), BF), ((4, ROWS, 128), BF), ((TOK, 128), BF)], flops=400_000_000,
    )(tokens, routes, gate_codes, cotangent, w_gate, w_up, w_down)
    gb, dp = call(
        expert_kernel, "expert", 2,
        [((4, 2, 4, ROWS, 128), BF), ((8, CAP, D), BF)],
        [buf(2, 8, CAP, D), buf(4, 8, ROWS, 128), pltpu.VMEM((4, D, 128), F32),
         dma(2), dma(13), dma(13), dma(9), dma(9)],
        collective=0, flops=3_500_000_000,
    )(x_own, w_own)
    fin, dpick = call(
        reduce_kernel, "reduce", 2,
        [((4, 2, 4, ROWS, 128), BF), ((CAP, D), BF)],
        [buf(4, CAP, D), buf(3, CAP, D), buf(3, CAP, D),
         buf(2, 2, ROWS, 128), buf(2, 2, ROWS, 128), buf(2, 2, ROWS, 128), buf(2, 2, ROWS, 128),
         buf(4, 2, ROWS, 128), buf(4, 2, ROWS, 128), buf(4, 2, ROWS, 128), buf(7, ROWS, 128),
         dma(13), dma(13), dma(4), dma(4), dma(19), dma(19)],
        collective=1,
    )(gb, dp.reshape(4, 2, CAP, D))
    return tuple(call(
        finish_kernel, "finish", 3,
        [((TOK, D), BF), ((ROWS, FF), F32), ((ROWS, FF), F32), ((ROWS, FF), F32)], flops=200_000_000,
    )(fin.reshape(8, 4, ROWS, 128), dpick, sel))


def solution(mesh):
    both, dom = P(("rep", "dom"), None), P("dom", None)
    return jax.shard_map(
        body,
        mesh=mesh,
        in_specs=(both, both, both, both, dom, dom, dom),
        out_specs=(both, dom, dom, dom),
        check_vma=False,
    )
```

```python
import jax
import jax.numpy as jnp
from jax import lax
from jax.experimental import pallas as pl
from jax.experimental.pallas import tpu as pltpu
from jax.sharding import PartitionSpec as P

D, FF, CAP, TOK = 1792, 1280, 96, 512
ROWS = 224
HALF = CAP // 2
MESH = pl.DeviceIdType.MESH
BF, F32 = jnp.bfloat16, jnp.float32
VMEM_LIMIT = 56 * 1024 * 1024
CHUNKS = ((0, 80), (80, 64), (144, 48), (192, 32))
NC = len(CHUNKS)

POS = {0: 0, 1: 1, 3: 2, 2: 3}


def coords():
    r, d = lax.axis_index("rep"), lax.axis_index("dom")
    return r // 8, (r // 2) % 4, r % 2, d // 4, d % 4


def dev(x, zh, c, zl, y):
    return (x * 8 + zh * 2 + c, zl * 4 + y)


def dot(a, b, dims=((1,), (0,))):
    return lax.dot_general(a, b, (dims, ((), ())), preferred_element_type=F32)


def iota(shape, axis):
    return lax.broadcasted_iota(jnp.int32, shape, axis)


def swiglu_back(g, u, dh):
    sig = 1.0 / (1.0 + jnp.exp(-g))
    act = g * sig
    return dh * u * sig * (1.0 + g * (1.0 - sig)), dh * act, act * u


def rows_of(xa, kind, lo, hi):
    return xa[kind, lo:hi].reshape((hi - lo) * CAP, D)


def forward_picked(lo, hi, xa, wa):
    part = lambda i: wa[i].reshape(D, 128)
    picked = rows_of(xa, 0, lo, hi)
    return dot(picked, jnp.concatenate([part(0), part(1)], axis=1)), dot(picked, part(3))


def forward_scaled(lo, hi, xa, wa, pre, rest, back):
    n = (hi - lo) * CAP
    part = lambda i: wa[i].reshape(D, 128)
    down = dot(rows_of(xa, 1, lo, hi), jnp.concatenate([part(2), part(3)], axis=1))
    lane = iota((n, 128), 1)
    rest = jnp.where(lane < 64, rest, down[:, 128:])
    dg, du, hid = swiglu_back(pre[:, :128], pre[:, 128:], down[:, :128])
    dg_r, du_r, hid_r = swiglu_back(rest, pltpu.roll(rest, 96, 1), pltpu.roll(rest, 64, 1))
    mix = jnp.where(lane < 32, dg_r, pltpu.roll(du_r, 32, 1))
    rest_p = jnp.where(lane < 64, mix, 0.0).astype(BF)
    rest_s = jnp.where((lane >= 64) & (lane < 96), pltpu.roll(hid_r, 64, 1), 0.0).astype(BF)
    up = jnp.concatenate([dg, du], axis=1).astype(BF)
    low = jnp.concatenate([hid.astype(BF), rest_s], axis=1)
    back[lo * CAP:hi * CAP, :256] = up
    back[lo * CAP:hi * CAP, 256:] = rest_p
    return up, low, rest_p


def terms_of(lo, hi, xa, at, up, low, rest_p):
    n = (hi - lo) * CAP
    first = ((0,), (0,))
    p_k = xa[0, lo:hi, :, pl.ds(at, 256)].reshape(n, 256)
    s_k = xa[1, lo:hi, :, pl.ds(at, 256)].reshape(n, 256)
    gu, hr, rr = dot(p_k, up, first), dot(s_k, low, first), dot(p_k, rest_p, first)
    return gu[:, :128], gu[:, 128:], hr[:, :128], hr[:, 128:] + rr


def expert_kernel(
    routes, codes, tok_hbm, cot_hbm, wg, wu, wd, fin, dpick, sel_out,
    tok, cot, tail, xa, wa, grad, gb, back, dp, dr, ds, df, ra, rb, ta, tb, low, high, zs, zr,
    local, ts, tr, ws, wr, gs, gr, es, er, ns, nr,
):
    x, zh, c, zl, y = coords()
    z, f = zh * 2 + zl, 2 * x + c
    sib = dev(x, zh, 1 - c, zl, y)
    ring = [dev((x + k) % 4, zh, c, zl, y) for k in (1, 2, 3)]
    right, left = ring[0], ring[2]
    yn, ys = (y + 1) % 4, (y + 3) % 4
    north, south = dev(x, zh, c, zl, yn), dev(x, zh, c, zl, ys)
    column = [dev(x, ((z + k) % 8) // 2, c, ((z + k) % 8) % 2, y) for k in range(1, 8)]
    pair = dev(x, zh, c, 1 - zl, y)
    partners = [sib, north, south] + ring + column

    barrier = pltpu.get_barrier_semaphore()
    for partner in partners:
        pl.semaphore_signal(barrier, inc=1, device_id=partner, device_id_type=MESH)

    dom, dom_z = zl * 4 + y, (1 - zl) * 4 + y
    tile = pl.multiple_of(f * 128, 128)
    last = pl.multiple_of(1024 + (f // 4) * 128, 128)
    loads = [
        pltpu.make_async_copy(tok_hbm, tok, local.at[0]),
        pltpu.make_async_copy(cot_hbm, cot, local.at[1]),
    ]
    for i, w in enumerate((wg, wu, wd)):
        loads.append(pltpu.make_async_copy(w.at[:, pl.ds(tile, 128)], wa.at[i, dom], local.at[2 + i]))
        loads.append(pltpu.make_async_copy(w.at[:, pl.ds(last, 128)], tail.at[i], local.at[5 + i]))
    for copy in loads:
        copy.start()

    sends = []

    def send(sems, index, src, dst, device):
        copy = pltpu.make_async_remote_copy(
            src_ref=src, dst_ref=dst, send_sem=sems[0].at[index], recv_sem=sems[1].at[index],
            device_id=device, device_id_type=MESH,
        )
        copy.start()
        sends.append(copy)
        return copy

    T, W, G, E, N = (ts, tr), (ws, wr), (gs, gr), (es, er), (ns, nr)
    slot = lambda delta, other: 2 * POS[delta] + other

    member = routes[...] == 0
    routed = jnp.max(jnp.where(member, 1.0, 0.0), axis=0, keepdims=True)
    code = jnp.sum(jnp.where(member, codes[...], 0), axis=0, keepdims=True).astype(F32)
    before = jnp.where(iota((TOK, TOK), 0) < iota((TOK, TOK), 1), 1.0, 0.0).astype(BF)
    rank = dot(jnp.broadcast_to(routed, (16, TOK)).astype(BF), before)[:1]
    hit = (jnp.broadcast_to(rank, (CAP, TOK)) == iota((CAP, TOK), 0).astype(F32)) & (
        jnp.broadcast_to(routed, (CAP, TOK)) > 0.0)
    sel = jnp.where(hit, 1.0, 0.0)
    weight = jnp.sum(sel * code, axis=1, keepdims=True) * (1.0 / 256.0)
    sel = sel.astype(BF)
    sel_out[...] = sel
    loads[0].wait()
    xa[0, 0] = dot(sel, tok[...]).astype(BF)
    pl.semaphore_wait(barrier, len(partners))
    p_right = send(T, 0, xa.at[0, 0], xa.at[0, slot(3, 0)], right)
    p_left = send(T, 1, xa.at[0, 0], xa.at[0, slot(1, 0)], left)
    loads[1].wait()
    xa[1, 0] = (weight * dot(sel, cot[...])).astype(BF)
    s_right = send(T, 2, xa.at[1, 0], xa.at[1, slot(3, 0)], right)
    s_left = send(T, 3, xa.at[1, 0], xa.at[1, slot(1, 0)], left)

    for copy in loads[2:]:
        copy.wait()
    rest = jnp.zeros((ROWS, 128), F32)
    src, dst = iota((128, 128), 0), iota((128, 128), 1)
    for part in range(3):
        move = (src - (f % 4) * 32 == dst - part * 32) & (dst // 32 == part)
        rest += dot(tail[part], jnp.where(move, 1.0, 0.0).astype(BF))
    wa[3, dom] = rest.astype(BF)
    mine = wa.at[:, dom]
    w_pair = send(W, 0, mine, mine, pair)
    w_north = send(W, 1, mine, mine, north)
    w_south = send(W, 2, mine, mine, south)
    x_sib = send(T, 4, xa.at[:, 0], xa.at[:, slot(0, 1)], sib)

    def onward(index, kind, delta):
        lo, device = (0, right) if delta == 3 else (HALF, left)
        return send(T, index, xa.at[kind, slot(delta, 0), lo:lo + HALF],
                    xa.at[kind, slot(2, 0), lo:lo + HALF], device)

    def share(index, kind, delta):
        return send(T, index, xa.at[kind, slot(delta, 0)], xa.at[kind, slot(delta, 1)], sib)

    def relay(index, base, up):
        block = wa.at[0:2, base + ys] if up else wa.at[2:4, base + yn]
        return send(W, index, block, block, north if up else south)

    w_pair.wait_recv()
    other = wa.at[:, dom_z]
    z_north, z_south = send(W, 3, other, other, north), send(W, 4, other, other, south)
    p_right.wait_recv()
    p_on_r, share_p3 = onward(5, 0, 3), share(9, 0, 3)
    p_left.wait_recv()
    p_on_l, share_p1 = onward(6, 0, 1), share(10, 0, 1)
    w_north.wait_recv()
    o_north = relay(5, zl * 4, True)
    w_south.wait_recv()
    o_south = relay(6, zl * 4, False)
    s_right.wait_recv()
    s_on_r, share_s3 = onward(7, 1, 3), share(11, 1, 3)
    s_left.wait_recv()
    s_on_l, share_s1 = onward(8, 1, 1), share(12, 1, 1)
    z_north.wait_recv()
    r_north = relay(7, (1 - zl) * 4, True)
    z_south.wait_recv()
    r_south = relay(8, (1 - zl) * 4, False)
    for copy in (o_north, o_south, r_north, r_south, x_sib, share_p3, share_p1, share_s3, share_s1):
        copy.wait_recv()

    up6 = forward_scaled(0, 6, xa, wa, *forward_picked(0, 6, xa, wa), back)
    p_on_r.wait_recv()
    p_on_l.wait_recv()
    share_p2 = share(13, 0, 2)

    def columns(k, carry):
        at = pl.multiple_of(k * 256, 256)
        for i, term in enumerate(terms_of(0, 6, xa, at, *up6)):
            grad[i, pl.ds(at, 256), :] = term
        return carry

    lax.fori_loop(0, D // 256, columns, 0)
    s_on_r.wait_recv()
    s_on_l.wait_recv()
    share_s2 = share(14, 1, 2)
    share_p2.wait_recv()
    pre = forward_picked(6, 8, xa, wa)
    share_s2.wait_recv()
    up2 = forward_scaled(6, 8, xa, wa, *pre, back)
    for k in range(D // 256):
        lo = k * 256
        for i, term in enumerate(terms_of(6, 8, xa, lo, *up2)):
            total = (grad[i, lo:lo + 256, :] + term).astype(BF)
            at = lo
            while at < lo + 256:
                d, r = at // ROWS, at % ROWS
                n = min(ROWS - r, lo + 256 - at)
                gb[i, d // 4, d % 4, r:r + n, :] = total[at - lo:at - lo + n]
                at += n

    f32 = lambda ref: ref.astype(F32)
    opposite = (y + 2) % 4
    opp, direct, added, z_sum, over_z, over_x, cores = ({} for _ in range(7))

    def rows(s):
        return pl.ds(*CHUNKS[s])

    def send_opposite(s):
        if s < NC:
            r = rows(s)
            opp[s] = (send(G, 13 * s, gb.at[0:2, :, opposite, r], ra.at[:, :, r], north),
                      send(G, 13 * s + 1, gb.at[2:4, :, opposite, r], rb.at[:, :, r], south))

    def send_direct(s):
        if s < NC:
            r = rows(s)
            direct[s] = (send(G, 13 * s + 2, gb.at[2:4, :, yn, r], low.at[2:4, :, r], north),
                         send(G, 13 * s + 3, gb.at[0:2, :, ys, r], high.at[0:2, :, r], south))

    def add_y(s):
        r = rows(s)
        opp[s][0].wait_recv()
        ta[:, :, r] = (f32(ra[:, :, r]) + f32(gb[0:2, :, yn, r])).astype(BF)
        add_n = send(G, 13 * s + 4, ta.at[:, :, r], low.at[0:2, :, r], north)
        opp[s][1].wait_recv()
        tb[:, :, r] = (f32(rb[:, :, r]) + f32(gb[2:4, :, ys, r])).astype(BF)
        added[s] = (add_n, send(G, 13 * s + 5, tb.at[:, :, r], high.at[2:4, :, r], south))
        send_direct(s + 1)
        send_opposite(s + 2)

    def sum_y(s):
        r = rows(s)
        for copy in direct[s] + added[s]:
            copy.wait_recv()
        zs[:, :, r] = (f32(gb[:, :, y, r]) + f32(low[:, :, r]) + f32(high[:, :, r])).astype(BF)
        z_sum[s] = []
        for k in (4, 3, 5, 2, 6, 1, 7):
            to = (z + k) % 8
            z_sum[s].append(send(G, 13 * s + 5 + k, zs.at[to // 2, to % 2, r], zr.at[k - 1, r],
                                 column[k - 1]))

    def to_ring(s, k, q):
        piece = fin.at[x, c, q, rows(s)]
        return [send(N, 19 * s + 3 + 3 * k + j - 1, piece, piece, ring[j - 1]) for j in (1, 2, 3)]

    def sum_z(s):
        r = rows(s)
        for copy in z_sum[s]:
            copy.wait_recv()
        total = f32(zs[zh, zl, r])
        for k in range(7):
            total += f32(zr[k, r])
        fin[x, c, zh, r] = total.astype(BF)
        piece = fin.at[x, c, zh, r]
        over_z[s] = [send(N, 19 * s + k - 1, piece, piece, dev(x, (zh + k) % 4, c, zl, y))
                     for k in (1, 2, 3)]
        over_x[s] = [to_ring(s, 0, zh)]

    def gather_z(s):
        for k in (1, 3, 2):
            over_z[s][k - 1].wait_recv()
            over_x[s].append(to_ring(s, k, (zh + 4 - k) % 4))
        block = fin.at[x, c, :, rows(s)]
        cores[s] = [send(N, 19 * s + 15, block, block, sib)]

    def gather_x(s):
        for j in (1, 3, 2):
            for copies in over_x[s]:
                copies[j - 1].wait_recv()
            block = fin.at[(x + 4 - j) % 4, c, :, rows(s)]
            cores[s].append(send(N, 19 * s + 15 + j, block, block, sib))

    send_opposite(0)
    send_direct(0)
    send_opposite(1)

    for k in range(D // 256):
        flat = jnp.concatenate([wa.at[i].reshape(D, 128)[k * 256:(k + 1) * 256] for i in (0, 1, 3)], axis=1)
        out = dot(back[...], flat, ((1,), (1,))).astype(BF)
        dp[:, :, :, k * 256:(k + 1) * 256] = out.reshape(4, 2, CAP, 256)
    d_sib = send(E, 0, dp.at[:, 1], dr, sib)

    stages = (add_y, sum_y, sum_z, gather_z, gather_x)
    d_ring = []
    for step in range(NC + len(stages) - 1):
        for lag, stage in enumerate(stages):
            if 0 <= step - lag < NC:
                stage(step - lag)
        if step == 0:
            d_sib.wait_recv()
            for k in (2, 1, 3):
                ds[k - 1] = (f32(dr[POS[k]]) + f32(dp[POS[k], 0])).astype(BF)
                d_ring.append(send(E, k, ds.at[k - 1], df.at[k - 1], ring[k - 1]))

    for copy in d_ring:
        copy.wait_recv()
    dpick[...] = (f32(dr[0]) + f32(dp[0, 0]) + f32(df[0]) + f32(df[1]) + f32(df[2])).astype(BF)
    for s in range(NC):
        for copy in cores[s]:
            copy.wait_recv()
    for copy in sends:
        copy.wait_send()


def finish_kernel(fin, dpick, sel, d_tokens, gg, gu, gd, rows, out_g, out_u, out_d, sems):
    copies = []

    def put(src, dst):
        copy = pltpu.make_async_copy(src, dst, sems.at[len(copies)])
        copy.start()
        copies.append(copy)

    lane = iota((ROWS, 128), 1)
    rest = [fin[f, 3].astype(F32) for f in range(8)]
    for part, (out, dst) in enumerate(((out_g, gg), (out_u, gu), (out_d, gd))):
        for f in range(8):
            out[:, f * 128:(f + 1) * 128] = fin[f, part].astype(F32)
        for half in range(2):
            total = jnp.zeros((ROWS, 128), F32)
            for k in range(4):
                shift = ((k - part) * 32) % 128
                tile = rest[4 * half + k]
                tile = pltpu.roll(tile, shift, 1) if shift else tile
                total = jnp.where(lane // 32 == k, tile, total)
            out[:, 1024 + half * 128:1152 + half * 128] = total
        put(out, dst)
    for k in range(4):
        at = pl.ds(k * 128, 128)
        rows[at] = dot(sel[:, at], dpick[...], ((0,), (0,))).astype(BF)
        put(rows.at[at], d_tokens.at[at])
    for copy in copies:
        copy.wait()


def call(kernel, name, ins, outs, scratch=(), collective=None, flops=0):
    extra = {} if collective is None else dict(collective_id=collective, has_side_effects=True)
    vmem, any_ = pl.BlockSpec(memory_space=pltpu.VMEM), pl.BlockSpec(memory_space=pl.ANY)
    return pl.pallas_call(
        kernel,
        name=name,
        out_shape=[jax.ShapeDtypeStruct(shape, dtype) for shape, dtype, _ in outs],
        in_specs=[vmem if inside else any_ for inside in ins],
        out_specs=[vmem if inside else any_ for _, _, inside in outs],
        scratch_shapes=list(scratch),
        cost_estimate=pl.CostEstimate(flops=flops, bytes_accessed=8_000_000, transcendentals=0),
        compiler_params=pltpu.CompilerParams(vmem_limit_bytes=VMEM_LIMIT, **extra),
    )


def body(tokens, routes, gate_codes, cotangent, w_gate, w_up, w_down):
    dma = lambda n: pltpu.SemaphoreType.DMA((n,))
    buf = lambda *shape: pltpu.VMEM(shape, BF)
    quarter = buf(2, 2, ROWS, 128)
    half = buf(4, 2, ROWS, 128)
    fin, dpick, sel = call(
        expert_kernel, "expert", (1, 1, 0, 0, 0, 0, 0),
        [((4, 2, 4, ROWS, 128), BF, 1), ((CAP, D), BF, 1), ((CAP, TOK), BF, 1)],
        [buf(TOK, D), buf(TOK, D), buf(3, ROWS, 128),
         buf(2, 8, CAP, D), buf(4, 8, ROWS, 128), pltpu.VMEM((4, D, 128), F32), buf(4, 2, 4, ROWS, 128),
         buf(8 * CAP, 384), buf(4, 2, CAP, D), buf(4, CAP, D), buf(3, CAP, D), buf(3, CAP, D),
         quarter, quarter, quarter, quarter, half, half, half, buf(7, ROWS, 128),
         dma(8), dma(15), dma(15), dma(9), dma(9), dma(13 * NC), dma(13 * NC), dma(4), dma(4),
         dma(19 * NC), dma(19 * NC)],
        collective=0, flops=4_000_000_000,
    )(routes.T, gate_codes.T, tokens, cotangent, w_gate, w_up, w_down)
    wide = pltpu.VMEM((ROWS, FF), F32)
    return tuple(call(
        finish_kernel, "finish", (1, 1, 1),
        [((TOK, D), BF, 0), ((ROWS, FF), F32, 0), ((ROWS, FF), F32, 0), ((ROWS, FF), F32, 0)],
        [buf(TOK, D), wide, wide, wide, dma(7)], flops=200_000_000,
    )(fin.reshape(8, 4, ROWS, 128), dpick, sel))


def solution(mesh):
    both, dom = P(("rep", "dom"), None), P("dom", None)
    return jax.shard_map(
        body,
        mesh=mesh,
        in_specs=(both, both, both, both, dom, dom, dom),
        out_specs=(both, dom, dom, dom),
        check_vma=False,
    )
```

```python
import jax
import jax.numpy as jnp
from jax import lax
from jax.experimental import pallas as pl
from jax.experimental.pallas import tpu as pltpu
from jax.sharding import PartitionSpec as P

D, FF, CAP, TOK = 1792, 1280, 96, 512
ROWS = 224
HALF = CAP // 2
MESH = pl.DeviceIdType.MESH
BF, F32 = jnp.bfloat16, jnp.float32
VMEM_LIMIT = 56 * 1024 * 1024
CHUNKS = (
    (0, 48, "z", "steps"),
    (48, 96, "relay", "steps"),
    (144, 48, "relay", "steps"),
    (192, 32, "direct", "once"),
)
NC = len(CHUNKS)
PLAN = (
    ("z_first", 0), ("opp", 1), ("near", 1), ("opp", 2), ("d_cores", 0),
    ("add", 1), ("near", 2), ("straight", 3), ("d_chips", 0), ("add", 2),
    ("z_sum", 0), ("sum_y", 1), ("sum_y", 2), ("y_sum", 0), ("sum_y", 3),
    ("sum_z", 1), ("onto_x", 0), ("sum_z", 2), ("onto_x", 1), ("sum_z", 3), ("onto_x", 2),
    ("onto_core", 0), ("onto_core", 1), ("onto_x", 3), ("onto_core", 2), ("onto_core", 3),
)

POS = {0: 0, 1: 1, 3: 2, 2: 3}


def coords():
    r, d = lax.axis_index("rep"), lax.axis_index("dom")
    return r // 8, (r // 2) % 4, r % 2, d // 4, d % 4


def dev(x, zh, c, zl, y):
    return (x * 8 + zh * 2 + c, zl * 4 + y)


def dot(a, b, dims=((1,), (0,))):
    return lax.dot_general(a, b, (dims, ((), ())), preferred_element_type=F32)


def iota(shape, axis):
    return lax.broadcasted_iota(jnp.int32, shape, axis)


def swiglu_back(g, u, dh):
    sig = 1.0 / (1.0 + jnp.exp(-g))
    act = g * sig
    return dh * u * sig * (1.0 + g * (1.0 - sig)), dh * act, act * u


def rows_of(xa, kind, lo, hi):
    return xa[kind, lo:hi].reshape((hi - lo) * CAP, D)


def forward_picked(lo, hi, xa, wa):
    part = lambda i: wa[i].reshape(D, 128)
    picked = rows_of(xa, 0, lo, hi)
    return dot(picked, jnp.concatenate([part(0), part(1)], axis=1)), dot(picked, part(3))


def forward_scaled(lo, hi, xa, wa, pre, rest, back):
    n = (hi - lo) * CAP
    part = lambda i: wa[i].reshape(D, 128)
    down = dot(rows_of(xa, 1, lo, hi), jnp.concatenate([part(2), part(3)], axis=1))
    lane = iota((n, 128), 1)
    rest = jnp.where(lane < 64, rest, down[:, 128:])
    dg, du, hid = swiglu_back(pre[:, :128], pre[:, 128:], down[:, :128])
    dg_r, du_r, hid_r = swiglu_back(rest, pltpu.roll(rest, 96, 1), pltpu.roll(rest, 64, 1))
    mix = jnp.where(lane < 32, dg_r, pltpu.roll(du_r, 32, 1))
    rest_p = jnp.where(lane < 64, mix, 0.0).astype(BF)
    rest_s = jnp.where((lane >= 64) & (lane < 96), pltpu.roll(hid_r, 64, 1), 0.0).astype(BF)
    up = jnp.concatenate([dg, du], axis=1).astype(BF)
    low = jnp.concatenate([hid.astype(BF), rest_s], axis=1)
    back[lo * CAP:hi * CAP, :256] = up
    back[lo * CAP:hi * CAP, 256:] = rest_p
    return up, low, rest_p


def terms_of(lo, hi, xa, at, up, low, rest_p):
    n = (hi - lo) * CAP
    first = ((0,), (0,))
    p_k = xa[0, lo:hi, :, pl.ds(at, 256)].reshape(n, 256)
    s_k = xa[1, lo:hi, :, pl.ds(at, 256)].reshape(n, 256)
    gu, hr, rr = dot(p_k, up, first), dot(s_k, low, first), dot(p_k, rest_p, first)
    return gu[:, :128], gu[:, 128:], hr[:, :128], hr[:, 128:] + rr


def expert_kernel(
    routes, codes, tok_hbm, cot_hbm, wg, wu, wd, fin, dpick, sel_out,
    tok, cot, tail, xa, wa, grad, gb, back, dp, dr, ds, df, ra, rb, ta, tb, low, mid, high, zs, zr, zw, zy, yr,
    local, ts, tr, ws, wr, gs, gr, es, er, ns, nr,
):
    x, zh, c, zl, y = coords()
    z, f = zh * 2 + zl, 2 * x + c
    sib = dev(x, zh, 1 - c, zl, y)
    ring = [dev((x + k) % 4, zh, c, zl, y) for k in (1, 2, 3)]
    right, left = ring[0], ring[2]
    yn, ys = (y + 1) % 4, (y + 3) % 4
    north, south = dev(x, zh, c, zl, yn), dev(x, zh, c, zl, ys)
    column = [dev(x, ((z + k) % 8) // 2, c, ((z + k) % 8) % 2, y) for k in range(1, 8)]
    pair = dev(x, zh, c, 1 - zl, y)
    partners = [sib, north, south] + ring + column

    barrier = pltpu.get_barrier_semaphore()
    for partner in partners:
        pl.semaphore_signal(barrier, inc=1, device_id=partner, device_id_type=MESH)

    dom, dom_z = zl * 4 + y, (1 - zl) * 4 + y
    tile = pl.multiple_of(f * 128, 128)
    last = pl.multiple_of(1024 + (f // 4) * 128, 128)
    loads = [
        pltpu.make_async_copy(tok_hbm, tok, local.at[0]),
        pltpu.make_async_copy(cot_hbm, cot, local.at[1]),
    ]
    for i, w in enumerate((wg, wu, wd)):
        loads.append(pltpu.make_async_copy(w.at[:, pl.ds(tile, 128)], wa.at[i, dom], local.at[2 + i]))
        loads.append(pltpu.make_async_copy(w.at[:, pl.ds(last, 128)], tail.at[i], local.at[5 + i]))
    for copy in loads:
        copy.start()

    sends = []

    def send(sems, index, src, dst, device):
        copy = pltpu.make_async_remote_copy(
            src_ref=src, dst_ref=dst, send_sem=sems[0].at[index], recv_sem=sems[1].at[index],
            device_id=device, device_id_type=MESH,
        )
        copy.start()
        sends.append(copy)
        return copy

    T, W, G, E, N = (ts, tr), (ws, wr), (gs, gr), (es, er), (ns, nr)
    slot = lambda delta, other: 2 * POS[delta] + other

    member = routes[...] == 0
    routed = jnp.max(jnp.where(member, 1.0, 0.0), axis=0, keepdims=True)
    code = jnp.sum(jnp.where(member, codes[...], 0), axis=0, keepdims=True).astype(F32)
    before = jnp.where(iota((TOK, TOK), 0) < iota((TOK, TOK), 1), 1.0, 0.0).astype(BF)
    rank = dot(jnp.broadcast_to(routed, (16, TOK)).astype(BF), before)[:1]
    hit = (jnp.broadcast_to(rank, (CAP, TOK)) == iota((CAP, TOK), 0).astype(F32)) & (
        jnp.broadcast_to(routed, (CAP, TOK)) > 0.0)
    sel = jnp.where(hit, 1.0, 0.0)
    weight = jnp.sum(sel * code, axis=1, keepdims=True) * (1.0 / 256.0)
    sel = sel.astype(BF)
    sel_out[...] = sel
    loads[0].wait()
    xa[0, 0] = dot(sel, tok[...]).astype(BF)
    pl.semaphore_wait(barrier, len(partners))
    p_right = send(T, 0, xa.at[0, 0], xa.at[0, slot(3, 0)], right)
    p_left = send(T, 1, xa.at[0, 0], xa.at[0, slot(1, 0)], left)
    loads[1].wait()
    xa[1, 0] = (weight * dot(sel, cot[...])).astype(BF)
    s_right = send(T, 2, xa.at[1, 0], xa.at[1, slot(3, 0)], right)
    s_left = send(T, 3, xa.at[1, 0], xa.at[1, slot(1, 0)], left)

    for copy in loads[2:]:
        copy.wait()
    rest = jnp.zeros((ROWS, 128), F32)
    src, dst = iota((128, 128), 0), iota((128, 128), 1)
    for part in range(3):
        move = (src - (f % 4) * 32 == dst - part * 32) & (dst // 32 == part)
        rest += dot(tail[part], jnp.where(move, 1.0, 0.0).astype(BF))
    wa[3, dom] = rest.astype(BF)
    mine = wa.at[:, dom]
    w_pair = send(W, 0, mine, mine, pair)
    w_north = send(W, 1, mine, mine, north)
    w_south = send(W, 2, mine, mine, south)
    x_sib = send(T, 4, xa.at[:, 0], xa.at[:, slot(0, 1)], sib)

    def onward(index, kind, delta):
        lo, device = (0, right) if delta == 3 else (HALF, left)
        return send(T, index, xa.at[kind, slot(delta, 0), lo:lo + HALF],
                    xa.at[kind, slot(2, 0), lo:lo + HALF], device)

    def share(index, kind, delta):
        return send(T, index, xa.at[kind, slot(delta, 0)], xa.at[kind, slot(delta, 1)], sib)

    def relay(index, base, up):
        block = wa.at[0:2, base + ys] if up else wa.at[2:4, base + yn]
        return send(W, index, block, block, north if up else south)

    w_pair.wait_recv()
    other = wa.at[:, dom_z]
    z_north, z_south = send(W, 3, other, other, north), send(W, 4, other, other, south)
    p_right.wait_recv()
    p_on_r, share_p3 = onward(5, 0, 3), share(9, 0, 3)
    p_left.wait_recv()
    p_on_l, share_p1 = onward(6, 0, 1), share(10, 0, 1)
    w_north.wait_recv()
    o_north = relay(5, zl * 4, True)
    w_south.wait_recv()
    o_south = relay(6, zl * 4, False)
    s_right.wait_recv()
    s_on_r, share_s3 = onward(7, 1, 3), share(11, 1, 3)
    s_left.wait_recv()
    s_on_l, share_s1 = onward(8, 1, 1), share(12, 1, 1)
    z_north.wait_recv()
    r_north = relay(7, (1 - zl) * 4, True)
    z_south.wait_recv()
    r_south = relay(8, (1 - zl) * 4, False)
    for copy in (o_north, o_south, r_north, r_south, x_sib, share_p3, share_p1, share_s3, share_s1):
        copy.wait_recv()

    up6 = forward_scaled(0, 6, xa, wa, *forward_picked(0, 6, xa, wa), back)
    p_on_r.wait_recv()
    p_on_l.wait_recv()
    share_p2 = share(13, 0, 2)

    def columns(k, carry):
        at = pl.multiple_of(k * 256, 256)
        for i, term in enumerate(terms_of(0, 6, xa, at, *up6)):
            grad[i, pl.ds(at, 256), :] = term
        return carry

    lax.fori_loop(0, D // 256, columns, 0)
    s_on_r.wait_recv()
    s_on_l.wait_recv()
    share_s2 = share(14, 1, 2)
    share_p2.wait_recv()
    pre = forward_picked(6, 8, xa, wa)
    share_s2.wait_recv()
    up2 = forward_scaled(6, 8, xa, wa, *pre, back)
    for k in range(D // 256):
        lo = k * 256
        for i, term in enumerate(terms_of(6, 8, xa, lo, *up2)):
            total = (grad[i, lo:lo + 256, :] + term).astype(BF)
            at = lo
            while at < lo + 256:
                d, r = at // ROWS, at % ROWS
                n = min(ROWS - r, lo + 256 - at)
                gb[i, d // 4, d % 4, r:r + n, :] = total[at - lo:at - lo + n]
                at += n

    f32 = lambda ref: ref.astype(F32)
    opposite = (y + 2) % 4
    ways = [dev(x, zh, c, zl, (y + k) % 4) for k in (1, 2, 3)]
    got = {}

    def rows(s):
        return pl.ds(CHUNKS[s][0], CHUNKS[s][1])

    def opp(s):
        r = rows(s)
        got[s, "opp"] = (send(G, 13 * s, gb.at[0:2, :, opposite, r], ra.at[:, :, r], north),
                         send(G, 13 * s + 1, gb.at[2:4, :, opposite, r], rb.at[:, :, r], south))

    def near(s):
        r = rows(s)
        got[s, "y"] = [send(G, 13 * s + 2, gb.at[2:4, :, yn, r], low.at[2:4, :, r], north),
                       send(G, 13 * s + 3, gb.at[0:2, :, ys, r], high.at[0:2, :, r], south)]

    def add(s):
        r = rows(s)
        got[s, "opp"][0].wait_recv()
        ta[:, :, r] = (f32(ra[:, :, r]) + f32(gb[0:2, :, yn, r])).astype(BF)
        got[s, "y"].append(send(G, 13 * s + 4, ta.at[:, :, r], low.at[0:2, :, r], north))
        got[s, "opp"][1].wait_recv()
        tb[:, :, r] = (f32(rb[:, :, r]) + f32(gb[2:4, :, ys, r])).astype(BF)
        got[s, "y"].append(send(G, 13 * s + 5, tb.at[:, :, r], high.at[2:4, :, r], south))

    def straight(s):
        r = rows(s)
        got[s, "y"] = [send(G, 13 * s + k, gb.at[:, :, (y + k) % 4, r], to.at[:, :, r], ways[k - 1])
                       for k, to in ((2, mid), (1, low), (3, high))]

    def sum_y(s):
        r = rows(s)
        for copy in got[s, "y"]:
            copy.wait_recv()
        total = f32(gb[:, :, y, r]) + f32(low[:, :, r]) + f32(high[:, :, r])
        if CHUNKS[s][2] == "direct":
            total += f32(mid[:, :, r])
        zs[:, :, r] = total.astype(BF)
        got[s, "z"] = []
        for k in (4, 3, 5, 2, 6, 1, 7):
            to = (z + k) % 8
            got[s, "z"].append(send(G, 13 * s + 5 + k, zs.at[to // 2, to % 2, r], zr.at[k - 1, r],
                                    column[k - 1]))

    def sum_z(s):
        r = rows(s)
        for copy in got[s, "z"]:
            copy.wait_recv()
        total = f32(zs[zh, zl, r])
        for k in range(7):
            total += f32(zr[k, r])
        fin[x, c, zh, r] = total.astype(BF)
        spread(s)

    def z_first(s):
        r = rows(s)
        got[s, "z"] = []
        for k in (4, 3, 5, 2, 6, 1, 7):
            to = (z + k) % 8
            got[s, "z"].append(send(G, 13 * s + 5 + k, gb.at[to // 2, to % 2, :, r], zw.at[k - 1, :, r],
                                    column[k - 1]))

    def z_sum(s):
        r = rows(s)
        for copy in got[s, "z"]:
            copy.wait_recv()
        total = f32(gb[zh, zl, :, r])
        for k in range(7):
            total += f32(zw[k, :, r])
        zy[:, r] = total.astype(BF)
        got[s, "y"] = [send(G, 13 * s + k, zy.at[(y + k) % 4, r], yr.at[k - 1, r], ways[k - 1])
                       for k in (2, 1, 3)]

    def y_sum(s):
        r = rows(s)
        for copy in got[s, "y"]:
            copy.wait_recv()
        fin[x, c, zh, r] = (f32(zy[y, r]) + f32(yr[0, r]) + f32(yr[1, r]) + f32(yr[2, r])).astype(BF)
        spread(s)

    def spread(s):
        piece = fin.at[x, c, zh, rows(s)]
        if CHUNKS[s][3] == "steps":
            got[s, "zh"] = [send(N, 19 * s + k - 1, piece, piece, dev(x, (zh + k) % 4, c, zl, y))
                            for k in (1, 2, 3)]
            got[s, "x"] = {(j, 0): send(N, 19 * s + 2 + j, piece, piece, ring[j - 1]) for j in (2, 1, 3)}
        else:
            got[s, "x"] = {}
            for j, k in ((2, 2), (1, 2), (3, 2), (2, 1), (2, 3), (0, 2), (1, 1), (1, 3), (3, 1), (3, 3),
                         (2, 0), (0, 1), (0, 3), (1, 0), (3, 0)):
                got[s, "x"][j, k] = send(N, 19 * s + 4 * k + j - 1, piece, piece,
                                         dev((x + j) % 4, (zh + k) % 4, c, zl, y))

    def onto_x(s):
        if CHUNKS[s][3] == "steps":
            for k in (1, 3, 2):
                got[s, "zh"][k - 1].wait_recv()
                piece = fin.at[x, c, (zh + 4 - k) % 4, rows(s)]
                for j in (2, 1, 3):
                    got[s, "x"][j, k] = send(N, 19 * s + 2 + 3 * k + j, piece, piece, ring[j - 1])
        else:
            for k in (1, 3, 2):
                got[s, "x"][0, k].wait_recv()
        block = fin.at[x, c, :, rows(s)]
        got[s, "core"] = [send(N, 19 * s + 15, block, block, sib)]

    def onto_core(s):
        for j in (1, 3, 2):
            for k in range(4):
                got[s, "x"][j, k].wait_recv()
            block = fin.at[(x + 4 - j) % 4, c, :, rows(s)]
            got[s, "core"].append(send(N, 19 * s + 15 + j, block, block, sib))

    def d_cores(_):
        for k in range(D // 256):
            flat = jnp.concatenate(
                [wa.at[i].reshape(D, 128)[k * 256:(k + 1) * 256] for i in (0, 1, 3)], axis=1)
            out = dot(back[...], flat, ((1,), (1,))).astype(BF)
            dp[:, :, :, k * 256:(k + 1) * 256] = out.reshape(4, 2, CAP, 256)
        got["d"] = send(E, 0, dp.at[:, 1], dr, sib)

    def d_chips(_):
        got["d"].wait_recv()
        for k in (2, 1, 3):
            ds[k - 1] = (f32(dr[POS[k]]) + f32(dp[POS[k], 0])).astype(BF)
            got["d", k] = send(E, k, ds.at[k - 1], df.at[k - 1], ring[k - 1])

    for stage, s in PLAN:
        dict(opp=opp, near=near, add=add, straight=straight, sum_y=sum_y, sum_z=sum_z, z_first=z_first,
             z_sum=z_sum, y_sum=y_sum, onto_x=onto_x, onto_core=onto_core, d_cores=d_cores,
             d_chips=d_chips)[stage](s)

    for k in (1, 2, 3):
        got["d", k].wait_recv()
    dpick[...] = (f32(dr[0]) + f32(dp[0, 0]) + f32(df[0]) + f32(df[1]) + f32(df[2])).astype(BF)
    for s in range(NC):
        for copy in got[s, "core"]:
            copy.wait_recv()
    for copy in sends:
        copy.wait_send()


def finish_kernel(fin, dpick, sel, d_tokens, gg, gu, gd, rows, out_g, out_u, out_d, sems):
    copies = []

    def put(src, dst):
        copy = pltpu.make_async_copy(src, dst, sems.at[len(copies)])
        copy.start()
        copies.append(copy)

    lane = iota((ROWS, 128), 1)
    rest = [fin[f, 3].astype(F32) for f in range(8)]
    for part, (out, dst) in enumerate(((out_g, gg), (out_u, gu), (out_d, gd))):
        for f in range(8):
            out[:, f * 128:(f + 1) * 128] = fin[f, part].astype(F32)
        for half in range(2):
            total = jnp.zeros((ROWS, 128), F32)
            for k in range(4):
                shift = ((k - part) * 32) % 128
                tile = rest[4 * half + k]
                tile = pltpu.roll(tile, shift, 1) if shift else tile
                total = jnp.where(lane // 32 == k, tile, total)
            out[:, 1024 + half * 128:1152 + half * 128] = total
        put(out, dst)
    for k in range(4):
        at = pl.ds(k * 128, 128)
        rows[at] = dot(sel[:, at], dpick[...], ((0,), (0,))).astype(BF)
        put(rows.at[at], d_tokens.at[at])
    for copy in copies:
        copy.wait()


def call(kernel, name, ins, outs, scratch=(), collective=None, flops=0):
    extra = {} if collective is None else dict(collective_id=collective, has_side_effects=True)
    vmem, any_ = pl.BlockSpec(memory_space=pltpu.VMEM), pl.BlockSpec(memory_space=pl.ANY)
    return pl.pallas_call(
        kernel,
        name=name,
        out_shape=[jax.ShapeDtypeStruct(shape, dtype) for shape, dtype, _ in outs],
        in_specs=[vmem if inside else any_ for inside in ins],
        out_specs=[vmem if inside else any_ for _, _, inside in outs],
        scratch_shapes=list(scratch),
        cost_estimate=pl.CostEstimate(flops=flops, bytes_accessed=8_000_000, transcendentals=0),
        compiler_params=pltpu.CompilerParams(vmem_limit_bytes=VMEM_LIMIT, **extra),
    )


def body(tokens, routes, gate_codes, cotangent, w_gate, w_up, w_down):
    dma = lambda n: pltpu.SemaphoreType.DMA((n,))
    buf = lambda *shape: pltpu.VMEM(shape, BF)
    quarter = buf(2, 2, ROWS, 128)
    half = buf(4, 2, ROWS, 128)
    fin, dpick, sel = call(
        expert_kernel, "expert", (1, 1, 0, 0, 0, 0, 0),
        [((4, 2, 4, ROWS, 128), BF, 1), ((CAP, D), BF, 1), ((CAP, TOK), BF, 1)],
        [buf(TOK, D), buf(TOK, D), buf(3, ROWS, 128),
         buf(2, 8, CAP, D), buf(4, 8, ROWS, 128), pltpu.VMEM((4, D, 128), F32), buf(4, 2, 4, ROWS, 128),
         buf(8 * CAP, 384), buf(4, 2, CAP, D), buf(4, CAP, D), buf(3, CAP, D), buf(3, CAP, D),
         quarter, quarter, quarter, quarter, half, half, half, half, buf(7, ROWS, 128),
         buf(7, 4, ROWS, 128), buf(4, ROWS, 128), buf(3, ROWS, 128),
         dma(8), dma(15), dma(15), dma(9), dma(9), dma(13 * NC), dma(13 * NC), dma(4), dma(4),
         dma(19 * NC), dma(19 * NC)],
        collective=0, flops=4_000_000_000,
    )(routes.T, gate_codes.T, tokens, cotangent, w_gate, w_up, w_down)
    wide = pltpu.VMEM((ROWS, FF), F32)
    return tuple(call(
        finish_kernel, "finish", (1, 1, 1),
        [((TOK, D), BF, 0), ((ROWS, FF), F32, 0), ((ROWS, FF), F32, 0), ((ROWS, FF), F32, 0)],
        [buf(TOK, D), wide, wide, wide, dma(7)], flops=200_000_000,
    )(fin.reshape(8, 4, ROWS, 128), dpick, sel))


def solution(mesh):
    both, dom = P(("rep", "dom"), None), P("dom", None)
    return jax.shard_map(
        body,
        mesh=mesh,
        in_specs=(both, both, both, both, dom, dom, dom),
        out_specs=(both, dom, dom, dom),
        check_vma=False,
    )
```

```python
import jax
import jax.numpy as jnp
from jax import lax
from jax.experimental import pallas as pl
from jax.experimental.pallas import tpu as pltpu
from jax.sharding import PartitionSpec as P

D, FF, CAP, TOK = 1792, 1280, 96, 512
ROWS = 224
HALF = CAP // 2
MESH = pl.DeviceIdType.MESH
BF, F32 = jnp.bfloat16, jnp.float32
VMEM_LIMIT = 56 * 1024 * 1024
CHUNKS = (
    (0, 48, "z", "steps"),
    (48, 96, "relay", "steps"),
    (144, 48, "relay", "steps"),
    (192, 32, "direct", "once"),
)
NC = len(CHUNKS)
PLAN = (
    ("z_first", 0), ("opp", 1), ("near", 1), ("opp", 2), ("d_cores", 0),
    ("add", 1), ("near", 2), ("straight", 3), ("d_chips", 0), ("add", 2),
    ("z_sum", 0), ("sum_y", 1), ("sum_y", 2), ("y_sum", 0), ("sum_y", 3),
    ("sum_z", 1), ("onto_x", 0), ("sum_z", 2), ("onto_x", 1), ("sum_z", 3), ("onto_x", 2),
    ("onto_core", 0), ("onto_core", 1), ("d_sum", 0), ("onto_x", 3), ("leave", 0), ("onto_core", 2),
    ("leave", 1), ("onto_core", 3), ("leave", 2), ("leave", 3),
)

POS = {0: 0, 1: 1, 3: 2, 2: 3}


def coords():
    r, d = lax.axis_index("rep"), lax.axis_index("dom")
    return r // 8, (r // 2) % 4, r % 2, d // 4, d % 4


def dev(x, zh, c, zl, y):
    return (x * 8 + zh * 2 + c, zl * 4 + y)


def dot(a, b, dims=((1,), (0,))):
    return lax.dot_general(a, b, (dims, ((), ())), preferred_element_type=F32)


def iota(shape, axis):
    return lax.broadcasted_iota(jnp.int32, shape, axis)


def swiglu_back(g, u, dh):
    sig = 1.0 / (1.0 + jnp.exp(-g))
    act = g * sig
    return dh * u * sig * (1.0 + g * (1.0 - sig)), dh * act, act * u


def rows_of(xa, kind, lo, hi):
    return xa[kind, lo:hi].reshape((hi - lo) * CAP, D)


def forward_picked(lo, hi, xa, wa):
    part = lambda i: wa[i].reshape(D, 128)
    picked = rows_of(xa, 0, lo, hi)
    return dot(picked, jnp.concatenate([part(0), part(1)], axis=1)), dot(picked, part(3))


def forward_scaled(lo, hi, xa, wa, pre, rest, back):
    n = (hi - lo) * CAP
    part = lambda i: wa[i].reshape(D, 128)
    down = dot(rows_of(xa, 1, lo, hi), jnp.concatenate([part(2), part(3)], axis=1))
    lane = iota((n, 128), 1)
    rest = jnp.where(lane < 64, rest, down[:, 128:])
    dg, du, hid = swiglu_back(pre[:, :128], pre[:, 128:], down[:, :128])
    dg_r, du_r, hid_r = swiglu_back(rest, pltpu.roll(rest, 96, 1), pltpu.roll(rest, 64, 1))
    mix = jnp.where(lane < 32, dg_r, pltpu.roll(du_r, 32, 1))
    rest_p = jnp.where(lane < 64, mix, 0.0).astype(BF)
    rest_s = jnp.where((lane >= 64) & (lane < 96), pltpu.roll(hid_r, 64, 1), 0.0).astype(BF)
    up = jnp.concatenate([dg, du], axis=1).astype(BF)
    low = jnp.concatenate([hid.astype(BF), rest_s], axis=1)
    back[lo * CAP:hi * CAP, :256] = up
    back[lo * CAP:hi * CAP, 256:] = rest_p
    return up, low, rest_p


def terms_of(lo, hi, xa, at, up, low, rest_p):
    n = (hi - lo) * CAP
    first = ((0,), (0,))
    p_k = xa[0, lo:hi, :, pl.ds(at, 256)].reshape(n, 256)
    s_k = xa[1, lo:hi, :, pl.ds(at, 256)].reshape(n, 256)
    gu, hr, rr = dot(p_k, up, first), dot(s_k, low, first), dot(p_k, rest_p, first)
    return gu[:, :128], gu[:, 128:], hr[:, :128], hr[:, 128:] + rr


def expert_kernel(
    routes, codes, tok_hbm, cot_hbm, wg, wu, wd, fin_hbm, dpick_hbm, sel_hbm,
    fin, dpick, sel_own, tok, cot, tail, xa, wa, grad, gb, back, dp, dr, ds, df, ra, rb, ta, tb, low, mid, high, zs, zr, zw, zy, yr,
    local, ts, tr, ws, wr, gs, gr, es, er, ns, nr,
):
    x, zh, c, zl, y = coords()
    z, f = zh * 2 + zl, 2 * x + c
    sib = dev(x, zh, 1 - c, zl, y)
    ring = [dev((x + k) % 4, zh, c, zl, y) for k in (1, 2, 3)]
    right, left = ring[0], ring[2]
    yn, ys = (y + 1) % 4, (y + 3) % 4
    north, south = dev(x, zh, c, zl, yn), dev(x, zh, c, zl, ys)
    column = [dev(x, ((z + k) % 8) // 2, c, ((z + k) % 8) % 2, y) for k in range(1, 8)]
    pair = dev(x, zh, c, 1 - zl, y)
    partners = [sib, north, south] + ring + column

    barrier = pltpu.get_barrier_semaphore()
    for partner in partners:
        pl.semaphore_signal(barrier, inc=1, device_id=partner, device_id_type=MESH)

    dom, dom_z = zl * 4 + y, (1 - zl) * 4 + y
    tile = pl.multiple_of(f * 128, 128)
    last = pl.multiple_of(1024 + (f // 4) * 128, 128)
    loads = [
        pltpu.make_async_copy(tok_hbm, tok, local.at[0]),
        pltpu.make_async_copy(cot_hbm, cot, local.at[1]),
    ]
    for i, w in enumerate((wg, wu, wd)):
        loads.append(pltpu.make_async_copy(w.at[:, pl.ds(tile, 128)], wa.at[i, dom], local.at[2 + i]))
        loads.append(pltpu.make_async_copy(w.at[:, pl.ds(last, 128)], tail.at[i], local.at[5 + i]))
    for copy in loads:
        copy.start()

    sends, outs = [], []

    def out(src, dst):
        copy = pltpu.make_async_copy(src, dst, local.at[8 + len(outs)])
        copy.start()
        outs.append(copy)

    def send(sems, index, src, dst, device):
        copy = pltpu.make_async_remote_copy(
            src_ref=src, dst_ref=dst, send_sem=sems[0].at[index], recv_sem=sems[1].at[index],
            device_id=device, device_id_type=MESH,
        )
        copy.start()
        sends.append(copy)
        return copy

    T, W, G, E, N = (ts, tr), (ws, wr), (gs, gr), (es, er), (ns, nr)
    slot = lambda delta, other: 2 * POS[delta] + other

    member = routes[...] == 0
    routed = jnp.max(jnp.where(member, 1.0, 0.0), axis=0, keepdims=True)
    code = jnp.sum(jnp.where(member, codes[...], 0), axis=0, keepdims=True).astype(F32)
    before = jnp.where(iota((TOK, TOK), 0) < iota((TOK, TOK), 1), 1.0, 0.0).astype(BF)
    rank = dot(jnp.broadcast_to(routed, (16, TOK)).astype(BF), before)[:1]
    hit = (jnp.broadcast_to(rank, (CAP, TOK)) == iota((CAP, TOK), 0).astype(F32)) & (
        jnp.broadcast_to(routed, (CAP, TOK)) > 0.0)
    sel = jnp.where(hit, 1.0, 0.0)
    weight = jnp.sum(sel * code, axis=1, keepdims=True) * (1.0 / 256.0)
    sel = sel.astype(BF)
    sel_own[...] = sel
    out(sel_own, sel_hbm)
    loads[0].wait()
    xa[0, 0] = dot(sel, tok[...]).astype(BF)
    for copy in loads[2:]:
        copy.wait()
    rest = jnp.zeros((ROWS, 128), F32)
    src, dst = iota((128, 128), 0), iota((128, 128), 1)
    for part in range(3):
        move = (src - (f % 4) * 32 == dst - part * 32) & (dst // 32 == part)
        rest += dot(tail[part], jnp.where(move, 1.0, 0.0).astype(BF))
    wa[3, dom] = rest.astype(BF)
    loads[1].wait()
    xa[1, 0] = (weight * dot(sel, cot[...])).astype(BF)

    def weights(index, half, dom_y, device):
        block = wa.at[2 * half:2 * half + 2, dom_y]
        return send(W, index, block, block, device)

    def onward(index, kind, delta):
        lo, device = (0, right) if delta == 3 else (HALF, left)
        return send(T, index, xa.at[kind, slot(delta, 0), lo:lo + HALF],
                    xa.at[kind, slot(2, 0), lo:lo + HALF], device)

    def share(index, kind, delta):
        return send(T, index, xa.at[kind, slot(delta, 0)], xa.at[kind, slot(delta, 1)], sib)

    here, there = zl * 4, (1 - zl) * 4
    pl.semaphore_wait(barrier, len(partners))
    p_right = send(T, 0, xa.at[0, 0], xa.at[0, slot(3, 0)], right)
    p_left = send(T, 1, xa.at[0, 0], xa.at[0, slot(1, 0)], left)
    north_0, south_1 = weights(0, 0, dom, north), weights(1, 1, dom, south)
    pair_0, pair_1 = weights(2, 0, dom, pair), weights(3, 1, dom, pair)
    north_1, south_0 = weights(4, 1, dom, north), weights(5, 0, dom, south)
    s_right = send(T, 2, xa.at[1, 0], xa.at[1, slot(3, 0)], right)
    s_left = send(T, 3, xa.at[1, 0], xa.at[1, slot(1, 0)], left)
    x_sib = send(T, 4, xa.at[:, 0], xa.at[:, slot(0, 1)], sib)

    north_0.wait_recv()
    all_w = [weights(6, 0, here + ys, north)]
    south_1.wait_recv()
    all_w.append(weights(7, 1, here + yn, south))
    pair_0.wait_recv()
    z_north_0 = weights(8, 0, dom_z, north)
    pair_1.wait_recv()
    z_south_1 = weights(9, 1, dom_z, south)
    all_w += [weights(10, 1, dom_z, north), weights(11, 0, dom_z, south), north_1, south_0]
    p_right.wait_recv()
    p_on_r, share_p3 = onward(5, 0, 3), share(9, 0, 3)
    p_left.wait_recv()
    p_on_l, share_p1 = onward(6, 0, 1), share(10, 0, 1)
    z_north_0.wait_recv()
    all_w.append(weights(12, 0, there + ys, north))
    z_south_1.wait_recv()
    all_w.append(weights(13, 1, there + yn, south))
    s_right.wait_recv()
    s_on_r, share_s3 = onward(7, 1, 3), share(11, 1, 3)
    s_left.wait_recv()
    s_on_l, share_s1 = onward(8, 1, 1), share(12, 1, 1)
    for copy in all_w + [x_sib, share_p3, share_p1, share_s3, share_s1]:
        copy.wait_recv()

    up6 = forward_scaled(0, 6, xa, wa, *forward_picked(0, 6, xa, wa), back)
    p_on_r.wait_recv()
    p_on_l.wait_recv()
    share_p2 = share(13, 0, 2)

    def columns(k, carry):
        at = pl.multiple_of(k * 256, 256)
        for i, term in enumerate(terms_of(0, 6, xa, at, *up6)):
            grad[i, pl.ds(at, 256), :] = term
        return carry

    lax.fori_loop(0, D // 256, columns, 0)
    s_on_r.wait_recv()
    s_on_l.wait_recv()
    share_s2 = share(14, 1, 2)
    share_p2.wait_recv()
    pre = forward_picked(6, 8, xa, wa)
    share_s2.wait_recv()
    up2 = forward_scaled(6, 8, xa, wa, *pre, back)
    for k in range(D // 256):
        lo = k * 256
        for i, term in enumerate(terms_of(6, 8, xa, lo, *up2)):
            total = (grad[i, lo:lo + 256, :] + term).astype(BF)
            at = lo
            while at < lo + 256:
                d, r = at // ROWS, at % ROWS
                n = min(ROWS - r, lo + 256 - at)
                gb[i, d // 4, d % 4, r:r + n, :] = total[at - lo:at - lo + n]
                at += n

    f32 = lambda ref: ref.astype(F32)
    opposite = (y + 2) % 4
    ways = [dev(x, zh, c, zl, (y + k) % 4) for k in (1, 2, 3)]
    got = {}

    def rows(s):
        return pl.ds(CHUNKS[s][0], CHUNKS[s][1])

    def opp(s):
        r = rows(s)
        got[s, "opp"] = (send(G, 13 * s, gb.at[0:2, :, opposite, r], ra.at[:, :, r], north),
                         send(G, 13 * s + 1, gb.at[2:4, :, opposite, r], rb.at[:, :, r], south))

    def near(s):
        r = rows(s)
        got[s, "y"] = [send(G, 13 * s + 2, gb.at[2:4, :, yn, r], low.at[2:4, :, r], north),
                       send(G, 13 * s + 3, gb.at[0:2, :, ys, r], high.at[0:2, :, r], south)]

    def add(s):
        r = rows(s)
        got[s, "opp"][0].wait_recv()
        ta[:, :, r] = (f32(ra[:, :, r]) + f32(gb[0:2, :, yn, r])).astype(BF)
        got[s, "y"].append(send(G, 13 * s + 4, ta.at[:, :, r], low.at[0:2, :, r], north))
        got[s, "opp"][1].wait_recv()
        tb[:, :, r] = (f32(rb[:, :, r]) + f32(gb[2:4, :, ys, r])).astype(BF)
        got[s, "y"].append(send(G, 13 * s + 5, tb.at[:, :, r], high.at[2:4, :, r], south))

    def straight(s):
        r = rows(s)
        got[s, "y"] = [send(G, 13 * s + k, gb.at[:, :, (y + k) % 4, r], to.at[:, :, r], ways[k - 1])
                       for k, to in ((2, mid), (1, low), (3, high))]

    def sum_y(s):
        r = rows(s)
        for copy in got[s, "y"]:
            copy.wait_recv()
        total = f32(gb[:, :, y, r]) + f32(low[:, :, r]) + f32(high[:, :, r])
        if CHUNKS[s][2] == "direct":
            total += f32(mid[:, :, r])
        zs[:, :, r] = total.astype(BF)
        got[s, "z"] = []
        for k in (4, 3, 5, 2, 6, 1, 7):
            to = (z + k) % 8
            got[s, "z"].append(send(G, 13 * s + 5 + k, zs.at[to // 2, to % 2, r], zr.at[k - 1, r],
                                    column[k - 1]))

    def sum_z(s):
        r = rows(s)
        for copy in got[s, "z"]:
            copy.wait_recv()
        total = f32(zs[zh, zl, r])
        for k in range(7):
            total += f32(zr[k, r])
        fin[x, c, zh, r] = total.astype(BF)
        spread(s)

    def z_first(s):
        r = rows(s)
        got[s, "z"] = []
        for k in (4, 3, 5, 2, 6, 1, 7):
            to = (z + k) % 8
            got[s, "z"].append(send(G, 13 * s + 5 + k, gb.at[to // 2, to % 2, :, r], zw.at[k - 1, :, r],
                                    column[k - 1]))

    def z_sum(s):
        r = rows(s)
        for copy in got[s, "z"]:
            copy.wait_recv()
        total = f32(gb[zh, zl, :, r])
        for k in range(7):
            total += f32(zw[k, :, r])
        zy[:, r] = total.astype(BF)
        got[s, "y"] = [send(G, 13 * s + k, zy.at[(y + k) % 4, r], yr.at[k - 1, r], ways[k - 1])
                       for k in (2, 1, 3)]

    def y_sum(s):
        r = rows(s)
        for copy in got[s, "y"]:
            copy.wait_recv()
        fin[x, c, zh, r] = (f32(zy[y, r]) + f32(yr[0, r]) + f32(yr[1, r]) + f32(yr[2, r])).astype(BF)
        spread(s)

    def spread(s):
        piece = fin.at[x, c, zh, rows(s)]
        if CHUNKS[s][3] == "steps":
            got[s, "zh"] = [send(N, 19 * s + k - 1, piece, piece, dev(x, (zh + k) % 4, c, zl, y))
                            for k in (1, 2, 3)]
            got[s, "x"] = {(j, 0): send(N, 19 * s + 2 + j, piece, piece, ring[j - 1]) for j in (2, 1, 3)}
        else:
            got[s, "x"] = {}
            for j, k in ((2, 2), (1, 2), (3, 2), (2, 1), (2, 3), (0, 2), (1, 1), (1, 3), (3, 1), (3, 3),
                         (2, 0), (0, 1), (0, 3), (1, 0), (3, 0)):
                got[s, "x"][j, k] = send(N, 19 * s + 4 * k + j - 1, piece, piece,
                                         dev((x + j) % 4, (zh + k) % 4, c, zl, y))

    def onto_x(s):
        if CHUNKS[s][3] == "steps":
            for k in (1, 3, 2):
                got[s, "zh"][k - 1].wait_recv()
                piece = fin.at[x, c, (zh + 4 - k) % 4, rows(s)]
                for j in (2, 1, 3):
                    got[s, "x"][j, k] = send(N, 19 * s + 2 + 3 * k + j, piece, piece, ring[j - 1])
        else:
            for k in (1, 3, 2):
                got[s, "x"][0, k].wait_recv()
        block = fin.at[x, c, :, rows(s)]
        got[s, "core"] = [send(N, 19 * s + 15, block, block, sib)]

    def onto_core(s):
        for j in (1, 3, 2):
            for k in range(4):
                got[s, "x"][j, k].wait_recv()
            block = fin.at[(x + 4 - j) % 4, c, :, rows(s)]
            got[s, "core"].append(send(N, 19 * s + 15 + j, block, block, sib))

    def d_cores(_):
        for k in range(D // 256):
            flat = jnp.concatenate(
                [wa.at[i].reshape(D, 128)[k * 256:(k + 1) * 256] for i in (0, 1, 3)], axis=1)
            out = dot(back[...], flat, ((1,), (1,))).astype(BF)
            dp[:, :, :, k * 256:(k + 1) * 256] = out.reshape(4, 2, CAP, 256)
        got["d"] = send(E, 0, dp.at[:, 1], dr, sib)

    def d_chips(_):
        got["d"].wait_recv()
        for k in (2, 1, 3):
            ds[k - 1] = (f32(dr[POS[k]]) + f32(dp[POS[k], 0])).astype(BF)
            got["d", k] = send(E, k, ds.at[k - 1], df.at[k - 1], ring[k - 1])

    def d_sum(_):
        for k in (1, 2, 3):
            got["d", k].wait_recv()
        total = f32(dr[0]) + f32(dp[0, 0]) + f32(df[0]) + f32(df[1]) + f32(df[2])
        dpick[...] = total.astype(BF)
        out(dpick, dpick_hbm)

    def leave(s):
        for copy in got[s, "core"]:
            copy.wait_recv()
        out(fin.at[:, :, :, rows(s)], fin_hbm.at[:, :, :, rows(s)])

    for stage, s in PLAN:
        dict(opp=opp, near=near, add=add, straight=straight, sum_y=sum_y, sum_z=sum_z, z_first=z_first,
             z_sum=z_sum, y_sum=y_sum, onto_x=onto_x, onto_core=onto_core, d_cores=d_cores,
             d_chips=d_chips, d_sum=d_sum, leave=leave)[stage](s)

    for copy in sends:
        copy.wait_send()
    for copy in outs:
        copy.wait()


def finish_kernel(fin_hbm, dpick_hbm, sel_hbm, d_tokens, gg, gu, gd,
                  fin, dpick, sel, rows, out_g, out_u, out_d, loaded, sems):
    loads = [pltpu.make_async_copy(sel_hbm, sel, loaded.at[4]),
             pltpu.make_async_copy(dpick_hbm, dpick, loaded.at[5])]
    parts = [pltpu.make_async_copy(fin_hbm.at[:, i], fin.at[:, i], loaded.at[i]) for i in range(4)]
    for copy in loads + [parts[i] for i in (3, 0, 1, 2)]:
        copy.start()
    copies = []

    def put(src, dst):
        copy = pltpu.make_async_copy(src, dst, sems.at[len(copies)])
        copy.start()
        copies.append(copy)

    for copy in loads:
        copy.wait()
    for k in range(4):
        at = pl.ds(k * 128, 128)
        rows[at] = dot(sel[:, at], dpick[...], ((0,), (0,))).astype(BF)
        put(rows.at[at], d_tokens.at[at])
    lane = iota((ROWS, 128), 1)
    parts[3].wait()
    rest = [fin[f, 3].astype(F32) for f in range(8)]
    for part, (out, dst) in enumerate(((out_g, gg), (out_u, gu), (out_d, gd))):
        parts[part].wait()
        for f in range(8):
            out[:, f * 128:(f + 1) * 128] = fin[f, part].astype(F32)
        for half in range(2):
            total = jnp.zeros((ROWS, 128), F32)
            for k in range(4):
                shift = ((k - part) * 32) % 128
                tile = rest[4 * half + k]
                tile = pltpu.roll(tile, shift, 1) if shift else tile
                total = jnp.where(lane // 32 == k, tile, total)
            out[:, 1024 + half * 128:1152 + half * 128] = total
        put(out, dst)
    for copy in copies:
        copy.wait()


def call(kernel, name, ins, outs, scratch=(), collective=None, flops=0):
    extra = {} if collective is None else dict(collective_id=collective, has_side_effects=True)
    vmem, any_ = pl.BlockSpec(memory_space=pltpu.VMEM), pl.BlockSpec(memory_space=pl.ANY)
    return pl.pallas_call(
        kernel,
        name=name,
        out_shape=[jax.ShapeDtypeStruct(shape, dtype) for shape, dtype, _ in outs],
        in_specs=[vmem if inside else any_ for inside in ins],
        out_specs=[vmem if inside else any_ for _, _, inside in outs],
        scratch_shapes=list(scratch),
        cost_estimate=pl.CostEstimate(flops=flops, bytes_accessed=8_000_000, transcendentals=0),
        compiler_params=pltpu.CompilerParams(vmem_limit_bytes=VMEM_LIMIT, **extra),
    )


def body(tokens, routes, gate_codes, cotangent, w_gate, w_up, w_down):
    dma = lambda n: pltpu.SemaphoreType.DMA((n,))
    buf = lambda *shape: pltpu.VMEM(shape, BF)
    quarter = buf(2, 2, ROWS, 128)
    half = buf(4, 2, ROWS, 128)
    fin, dpick, sel = call(
        expert_kernel, "expert", (1, 1, 0, 0, 0, 0, 0),
        [((4, 2, 4, ROWS, 128), BF, 0), ((CAP, D), BF, 0), ((CAP, TOK), BF, 0)],
        [buf(4, 2, 4, ROWS, 128), buf(CAP, D), buf(CAP, TOK), buf(TOK, D), buf(TOK, D), buf(3, ROWS, 128),
         buf(2, 8, CAP, D), buf(4, 8, ROWS, 128), pltpu.VMEM((4, D, 128), F32), buf(4, 2, 4, ROWS, 128),
         buf(8 * CAP, 384), buf(4, 2, CAP, D), buf(4, CAP, D), buf(3, CAP, D), buf(3, CAP, D),
         quarter, quarter, quarter, quarter, half, half, half, half, buf(7, ROWS, 128),
         buf(7, 4, ROWS, 128), buf(4, ROWS, 128), buf(3, ROWS, 128),
         dma(10 + NC), dma(15), dma(15), dma(14), dma(14), dma(13 * NC), dma(13 * NC), dma(4), dma(4),
         dma(19 * NC), dma(19 * NC)],
        collective=0, flops=4_000_000_000,
    )(routes.T, gate_codes.T, tokens, cotangent, w_gate, w_up, w_down)
    wide = pltpu.VMEM((ROWS, FF), F32)
    return tuple(call(
        finish_kernel, "finish", (0, 0, 0),
        [((TOK, D), BF, 0), ((ROWS, FF), F32, 0), ((ROWS, FF), F32, 0), ((ROWS, FF), F32, 0)],
        [buf(8, 4, ROWS, 128), buf(CAP, D), buf(CAP, TOK), buf(TOK, D), wide, wide, wide, dma(6), dma(7)], flops=200_000_000,
    )(fin.reshape(8, 4, ROWS, 128), dpick, sel))


def solution(mesh):
    both, dom = P(("rep", "dom"), None), P("dom", None)
    return jax.shard_map(
        body,
        mesh=mesh,
        in_specs=(both, both, both, both, dom, dom, dom),
        out_specs=(both, dom, dom, dom),
        check_vma=False,
    )
```

```python
import jax
import jax.numpy as jnp
from jax import lax
from jax.experimental import pallas as pl
from jax.experimental.pallas import tpu as pltpu
from jax.sharding import PartitionSpec as P

D, FF, CAP, TOK = 1792, 1280, 96, 512
ROWS = 224
HALF = CAP // 2
MESH = pl.DeviceIdType.MESH
BF, F32 = jnp.bfloat16, jnp.float32
VMEM_LIMIT = 56 * 1024 * 1024
CHUNKS = (
    (0, 48, "z", "steps"),
    (48, 48, "relay", "steps"),
    (96, 64, "relay", "steps"),
    (160, 32, "relay", "steps"),
    (192, 32, "relay", "once"),
)
NC = len(CHUNKS)
PLAN = (
    ("z_first", 0), ("opp", 1), ("near", 1), ("opp", 2), ("d_cores", 0), ("add", 1), ("near", 2), ("opp", 3),
    ("d_chips", 0), ("add", 2), ("near", 3), ("opp", 4), ("sum_y", 1), ("add", 3), ("near", 4), ("sum_y", 2),
    ("add", 4), ("z_sum", 0), ("sum_y", 3), ("sum_z", 1), ("sum_y", 4), ("y_sum", 0), ("sum_z", 2),
    ("sum_z", 3), ("onto_x", 1), ("sum_z", 4), ("onto_x", 0), ("d_sum", 0), ("onto_x", 2), ("onto_x", 3),
    ("onto_core", 1), ("leave", 1), ("onto_core", 0), ("onto_x", 4), ("onto_core", 4), ("leave", 0),
    ("onto_core", 2), ("leave", 4), ("onto_core", 3), ("leave", 2), ("leave", 3),
)

POS = {0: 0, 1: 1, 3: 2, 2: 3}


def coords():
    r, d = lax.axis_index("rep"), lax.axis_index("dom")
    return r // 8, (r // 2) % 4, r % 2, d // 4, d % 4


def dev(x, zh, c, zl, y):
    return (x * 8 + zh * 2 + c, zl * 4 + y)


def dot(a, b, dims=((1,), (0,))):
    return lax.dot_general(a, b, (dims, ((), ())), preferred_element_type=F32)


def iota(shape, axis):
    return lax.broadcasted_iota(jnp.int32, shape, axis)


def swiglu_back(g, u, dh):
    sig = 1.0 / (1.0 + jnp.exp(-g))
    act = g * sig
    return dh * u * sig * (1.0 + g * (1.0 - sig)), dh * act, act * u


def rows_of(xa, kind, lo, hi):
    return xa[kind, lo:hi].reshape((hi - lo) * CAP, D)


def forward_picked(lo, hi, xa, wa):
    part = lambda i: wa[i].reshape(D, 128)
    picked = rows_of(xa, 0, lo, hi)
    return dot(picked, jnp.concatenate([part(0), part(1)], axis=1)), dot(picked, part(3))


def forward_scaled(lo, hi, xa, wa, pre, rest, back):
    n = (hi - lo) * CAP
    part = lambda i: wa[i].reshape(D, 128)
    down = dot(rows_of(xa, 1, lo, hi), jnp.concatenate([part(2), part(3)], axis=1))
    lane = iota((n, 128), 1)
    rest = jnp.where(lane < 64, rest, down[:, 128:])
    dg, du, hid = swiglu_back(pre[:, :128], pre[:, 128:], down[:, :128])
    dg_r, du_r, hid_r = swiglu_back(rest, pltpu.roll(rest, 96, 1), pltpu.roll(rest, 64, 1))
    mix = jnp.where(lane < 32, dg_r, pltpu.roll(du_r, 32, 1))
    rest_p = jnp.where(lane < 64, mix, 0.0).astype(BF)
    rest_s = jnp.where((lane >= 64) & (lane < 96), pltpu.roll(hid_r, 64, 1), 0.0).astype(BF)
    up = jnp.concatenate([dg, du], axis=1).astype(BF)
    low = jnp.concatenate([hid.astype(BF), rest_s], axis=1)
    back[lo * CAP:hi * CAP, :256] = up
    back[lo * CAP:hi * CAP, 256:] = rest_p
    return up, low, rest_p


def terms_of(lo, hi, xa, at, up, low, rest_p):
    n = (hi - lo) * CAP
    first = ((0,), (0,))
    p_k = xa[0, lo:hi, :, pl.ds(at, 256)].reshape(n, 256)
    s_k = xa[1, lo:hi, :, pl.ds(at, 256)].reshape(n, 256)
    gu, hr, rr = dot(p_k, up, first), dot(s_k, low, first), dot(p_k, rest_p, first)
    return gu[:, :128], gu[:, 128:], hr[:, :128], hr[:, 128:] + rr


def expert_kernel(
    routes, codes, tok_hbm, cot_hbm, wg, wu, wd, fin_hbm, dpick_hbm, sel_hbm,
    fin, dpick, sel_own, tok, cot, tail, xa, wa, grad, gb, back, dp, dr, ds, df, ra, rb, ta, tb, low, mid, high, zs, zr, zw, zy, yr,
    local, ts, tr, ws, wr, gs, gr, es, er, ns, nr, told,
):
    x, zh, c, zl, y = coords()
    z, f = zh * 2 + zl, 2 * x + c
    sib = dev(x, zh, 1 - c, zl, y)
    ring = [dev((x + k) % 4, zh, c, zl, y) for k in (1, 2, 3)]
    right, left = ring[0], ring[2]
    yn, ys = (y + 1) % 4, (y + 3) % 4
    north, south = dev(x, zh, c, zl, yn), dev(x, zh, c, zl, ys)
    column = [dev(x, ((z + k) % 8) // 2, c, ((z + k) % 8) % 2, y) for k in range(1, 8)]
    pair = dev(x, zh, c, 1 - zl, y)
    nearby = [right, left, north, south, column[0], column[6]]
    partners = [sib] + nearby

    barrier = pltpu.get_barrier_semaphore()
    for partner in partners:
        pl.semaphore_signal(barrier, inc=1, device_id=partner, device_id_type=MESH)

    dom, dom_z = zl * 4 + y, (1 - zl) * 4 + y
    tile = pl.multiple_of(f * 128, 128)
    last = pl.multiple_of(1024 + (f // 4) * 128, 128)
    loads = [
        pltpu.make_async_copy(tok_hbm, tok, local.at[0]),
        pltpu.make_async_copy(cot_hbm, cot, local.at[1]),
    ]
    for i, w in enumerate((wg, wu, wd)):
        loads.append(pltpu.make_async_copy(w.at[:, pl.ds(tile, 128)], wa.at[i, dom], local.at[2 + i]))
        loads.append(pltpu.make_async_copy(w.at[:, pl.ds(last, 128)], tail.at[i], local.at[5 + i]))
    for copy in loads:
        copy.start()

    sends, outs = [], []

    def out(src, dst):
        copy = pltpu.make_async_copy(src, dst, local.at[8 + len(outs)])
        copy.start()
        outs.append(copy)

    def send(sems, index, src, dst, device):
        copy = pltpu.make_async_remote_copy(
            src_ref=src, dst_ref=dst, send_sem=sems[0].at[index], recv_sem=sems[1].at[index],
            device_id=device, device_id_type=MESH,
        )
        copy.start()
        sends.append(copy)
        return copy

    T, W, G, E, N = (ts, tr), (ws, wr), (gs, gr), (es, er), (ns, nr)
    slot = lambda delta, other: 2 * POS[delta] + other

    member = routes[...] == 0
    routed = jnp.max(jnp.where(member, 1.0, 0.0), axis=0, keepdims=True)
    code = jnp.sum(jnp.where(member, codes[...], 0), axis=0, keepdims=True).astype(F32)
    before = jnp.where(iota((TOK, TOK), 0) < iota((TOK, TOK), 1), 1.0, 0.0).astype(BF)
    rank = dot(jnp.broadcast_to(routed, (16, TOK)).astype(BF), before)[:1]
    hit = (jnp.broadcast_to(rank, (CAP, TOK)) == iota((CAP, TOK), 0).astype(F32)) & (
        jnp.broadcast_to(routed, (CAP, TOK)) > 0.0)
    sel = jnp.where(hit, 1.0, 0.0)
    weight = jnp.sum(sel * code, axis=1, keepdims=True) * (1.0 / 256.0)
    sel = sel.astype(BF)
    sel_own[...] = sel
    out(sel_own, sel_hbm)
    loads[0].wait()
    xa[0, 0] = dot(sel, tok[...]).astype(BF)
    for copy in loads[2:]:
        copy.wait()
    rest = jnp.zeros((ROWS, 128), F32)
    src, dst = iota((128, 128), 0), iota((128, 128), 1)
    for part in range(3):
        move = (src - (f % 4) * 32 == dst - part * 32) & (dst // 32 == part)
        rest += dot(tail[part], jnp.where(move, 1.0, 0.0).astype(BF))
    wa[3, dom] = rest.astype(BF)
    loads[1].wait()
    xa[1, 0] = (weight * dot(sel, cot[...])).astype(BF)

    def weights(index, half, dom_y, device):
        block = wa.at[2 * half:2 * half + 2, dom_y]
        return send(W, index, block, block, device)

    def onward(index, kind, delta):
        lo, device = (0, right) if delta == 3 else (HALF, left)
        return send(T, index, xa.at[kind, slot(delta, 0), lo:lo + HALF],
                    xa.at[kind, slot(2, 0), lo:lo + HALF], device)

    def share(index, kind, delta):
        return send(T, index, xa.at[kind, slot(delta, 0)], xa.at[kind, slot(delta, 1)], sib)

    def tell(index, devices):
        for device in devices:
            pl.semaphore_signal(told.at[index], inc=1, device_id=device, device_id_type=MESH)

    here, there = zl * 4, (1 - zl) * 4
    pl.semaphore_wait(barrier, len(partners))
    p_right = send(T, 0, xa.at[0, 0], xa.at[0, slot(3, 0)], right)
    p_left = send(T, 1, xa.at[0, 0], xa.at[0, slot(1, 0)], left)
    north_0, south_1 = weights(0, 0, dom, north), weights(1, 1, dom, south)
    pair_0, pair_1 = weights(2, 0, dom, pair), weights(3, 1, dom, pair)
    north_1, south_0 = weights(4, 1, dom, north), weights(5, 0, dom, south)
    s_right = send(T, 2, xa.at[1, 0], xa.at[1, slot(3, 0)], right)
    s_left = send(T, 3, xa.at[1, 0], xa.at[1, slot(1, 0)], left)
    x_sib = send(T, 4, xa.at[:, 0], xa.at[:, slot(0, 1)], sib)

    tell(0, nearby)
    north_0.wait_recv()
    all_w = [weights(6, 0, here + ys, north)]
    south_1.wait_recv()
    all_w.append(weights(7, 1, here + yn, south))
    pair_0.wait_recv()
    z_north_0 = weights(8, 0, dom_z, north)
    pair_1.wait_recv()
    z_south_1 = weights(9, 1, dom_z, south)
    all_w += [weights(10, 1, dom_z, north), weights(11, 0, dom_z, south), north_1, south_0]
    pl.semaphore_wait(told.at[0], len(nearby))
    tell(1, (column[0], column[6]))
    p_right.wait_recv()
    p_on_r, share_p3 = onward(5, 0, 3), share(9, 0, 3)
    p_left.wait_recv()
    p_on_l, share_p1 = onward(6, 0, 1), share(10, 0, 1)
    z_north_0.wait_recv()
    all_w.append(weights(12, 0, there + ys, north))
    z_south_1.wait_recv()
    all_w.append(weights(13, 1, there + yn, south))
    pl.semaphore_wait(told.at[1], 2)
    tell(2, (column[0], column[6]))
    s_right.wait_recv()
    s_on_r, share_s3 = onward(7, 1, 3), share(11, 1, 3)
    s_left.wait_recv()
    s_on_l, share_s1 = onward(8, 1, 1), share(12, 1, 1)
    pl.semaphore_wait(told.at[2], 2)
    for copy in all_w + [x_sib, share_p3, share_p1, share_s3, share_s1]:
        copy.wait_recv()

    up6 = forward_scaled(0, 6, xa, wa, *forward_picked(0, 6, xa, wa), back)
    p_on_r.wait_recv()
    p_on_l.wait_recv()
    share_p2 = share(13, 0, 2)

    def columns(k, carry):
        at = pl.multiple_of(k * 256, 256)
        for i, term in enumerate(terms_of(0, 6, xa, at, *up6)):
            grad[i, pl.ds(at, 256), :] = term
        return carry

    lax.fori_loop(0, D // 256, columns, 0)
    s_on_r.wait_recv()
    s_on_l.wait_recv()
    share_s2 = share(14, 1, 2)
    share_p2.wait_recv()
    pre = forward_picked(6, 8, xa, wa)
    share_s2.wait_recv()
    up2 = forward_scaled(6, 8, xa, wa, *pre, back)
    for k in range(D // 256):
        lo = k * 256
        for i, term in enumerate(terms_of(6, 8, xa, lo, *up2)):
            total = (grad[i, lo:lo + 256, :] + term).astype(BF)
            at = lo
            while at < lo + 256:
                d, r = at // ROWS, at % ROWS
                n = min(ROWS - r, lo + 256 - at)
                gb[i, d // 4, d % 4, r:r + n, :] = total[at - lo:at - lo + n]
                at += n

    f32 = lambda ref: ref.astype(F32)
    opposite = (y + 2) % 4
    ways = [dev(x, zh, c, zl, (y + k) % 4) for k in (1, 2, 3)]
    got = {}

    def rows(s):
        return pl.ds(CHUNKS[s][0], CHUNKS[s][1])

    def opp(s):
        r = rows(s)
        got[s, "opp"] = (send(G, 13 * s, gb.at[0:2, :, opposite, r], ra.at[:, :, r], north),
                         send(G, 13 * s + 1, gb.at[2:4, :, opposite, r], rb.at[:, :, r], south))

    def near(s):
        r = rows(s)
        got[s, "y"] = [send(G, 13 * s + 2, gb.at[2:4, :, yn, r], low.at[2:4, :, r], north),
                       send(G, 13 * s + 3, gb.at[0:2, :, ys, r], high.at[0:2, :, r], south)]

    def add(s):
        r = rows(s)
        got[s, "opp"][0].wait_recv()
        ta[:, :, r] = (f32(ra[:, :, r]) + f32(gb[0:2, :, yn, r])).astype(BF)
        got[s, "y"].append(send(G, 13 * s + 4, ta.at[:, :, r], low.at[0:2, :, r], north))
        got[s, "opp"][1].wait_recv()
        tb[:, :, r] = (f32(rb[:, :, r]) + f32(gb[2:4, :, ys, r])).astype(BF)
        got[s, "y"].append(send(G, 13 * s + 5, tb.at[:, :, r], high.at[2:4, :, r], south))

    def straight(s):
        r = rows(s)
        got[s, "y"] = [send(G, 13 * s + k, gb.at[:, :, (y + k) % 4, r], to.at[:, :, r], ways[k - 1])
                       for k, to in ((2, mid), (1, low), (3, high))]

    def sum_y(s):
        r = rows(s)
        for copy in got[s, "y"]:
            copy.wait_recv()
        total = f32(gb[:, :, y, r]) + f32(low[:, :, r]) + f32(high[:, :, r])
        if CHUNKS[s][2] == "direct":
            total += f32(mid[:, :, r])
        zs[:, :, r] = total.astype(BF)
        got[s, "z"] = []
        for k in (4, 3, 5, 2, 6, 1, 7):
            to = (z + k) % 8
            got[s, "z"].append(send(G, 13 * s + 5 + k, zs.at[to // 2, to % 2, r], zr.at[k - 1, r],
                                    column[k - 1]))

    def sum_z(s):
        r = rows(s)
        for copy in got[s, "z"]:
            copy.wait_recv()
        total = f32(zs[zh, zl, r])
        for k in range(7):
            total += f32(zr[k, r])
        fin[x, c, zh, r] = total.astype(BF)
        spread(s)

    def z_first(s):
        r = rows(s)
        got[s, "z"] = []
        for k in (4, 3, 5, 2, 6, 1, 7):
            to = (z + k) % 8
            got[s, "z"].append(send(G, 13 * s + 5 + k, gb.at[to // 2, to % 2, :, r], zw.at[k - 1, :, r],
                                    column[k - 1]))

    def z_sum(s):
        r = rows(s)
        for copy in got[s, "z"]:
            copy.wait_recv()
        total = f32(gb[zh, zl, :, r])
        for k in range(7):
            total += f32(zw[k, :, r])
        zy[:, r] = total.astype(BF)
        got[s, "y"] = [send(G, 13 * s + k, zy.at[(y + k) % 4, r], yr.at[k - 1, r], ways[k - 1])
                       for k in (2, 1, 3)]

    def y_sum(s):
        r = rows(s)
        for copy in got[s, "y"]:
            copy.wait_recv()
        fin[x, c, zh, r] = (f32(zy[y, r]) + f32(yr[0, r]) + f32(yr[1, r]) + f32(yr[2, r])).astype(BF)
        spread(s)

    def spread(s):
        piece = fin.at[x, c, zh, rows(s)]
        if CHUNKS[s][3] == "steps":
            got[s, "zh"] = [send(N, 19 * s + k - 1, piece, piece, dev(x, (zh + k) % 4, c, zl, y))
                            for k in (1, 2, 3)]
            got[s, "x"] = {(j, 0): send(N, 19 * s + 2 + j, piece, piece, ring[j - 1]) for j in (2, 1, 3)}
        else:
            got[s, "x"] = {}
            for j, k in ((2, 2), (1, 2), (3, 2), (2, 1), (2, 3), (0, 2), (1, 1), (1, 3), (3, 1), (3, 3),
                         (2, 0), (0, 1), (0, 3), (1, 0), (3, 0)):
                got[s, "x"][j, k] = send(N, 19 * s + 4 * k + j - 1, piece, piece,
                                         dev((x + j) % 4, (zh + k) % 4, c, zl, y))

    def onto_x(s):
        if CHUNKS[s][3] == "steps":
            for k in (1, 3, 2):
                got[s, "zh"][k - 1].wait_recv()
                piece = fin.at[x, c, (zh + 4 - k) % 4, rows(s)]
                for j in (2, 1, 3):
                    got[s, "x"][j, k] = send(N, 19 * s + 2 + 3 * k + j, piece, piece, ring[j - 1])
        else:
            for k in (1, 3, 2):
                got[s, "x"][0, k].wait_recv()
        block = fin.at[x, c, :, rows(s)]
        got[s, "core"] = [send(N, 19 * s + 15, block, block, sib)]

    def onto_core(s):
        for j in (1, 3, 2):
            for k in range(4):
                got[s, "x"][j, k].wait_recv()
            block = fin.at[(x + 4 - j) % 4, c, :, rows(s)]
            got[s, "core"].append(send(N, 19 * s + 15 + j, block, block, sib))

    def d_cores(_):
        for k in range(D // 256):
            flat = jnp.concatenate(
                [wa.at[i].reshape(D, 128)[k * 256:(k + 1) * 256] for i in (0, 1, 3)], axis=1)
            out = dot(back[...], flat, ((1,), (1,))).astype(BF)
            dp[:, :, :, k * 256:(k + 1) * 256] = out.reshape(4, 2, CAP, 256)
        got["d"] = send(E, 0, dp.at[:, 1], dr, sib)

    def d_chips(_):
        got["d"].wait_recv()
        for k in (2, 1, 3):
            ds[k - 1] = (f32(dr[POS[k]]) + f32(dp[POS[k], 0])).astype(BF)
            got["d", k] = send(E, k, ds.at[k - 1], df.at[k - 1], ring[k - 1])

    def d_sum(_):
        for k in (1, 2, 3):
            got["d", k].wait_recv()
        total = f32(dr[0]) + f32(dp[0, 0]) + f32(df[0]) + f32(df[1]) + f32(df[2])
        dpick[...] = total.astype(BF)
        out(dpick, dpick_hbm)

    def leave(s):
        for copy in got[s, "core"]:
            copy.wait_recv()
        out(fin.at[:, :, :, rows(s)], fin_hbm.at[:, :, :, rows(s)])

    for stage, s in PLAN:
        dict(opp=opp, near=near, add=add, straight=straight, sum_y=sum_y, sum_z=sum_z, z_first=z_first,
             z_sum=z_sum, y_sum=y_sum, onto_x=onto_x, onto_core=onto_core, d_cores=d_cores,
             d_chips=d_chips, d_sum=d_sum, leave=leave)[stage](s)

    for copy in sends:
        copy.wait_send()
    for copy in outs:
        copy.wait()


def finish_kernel(fin_hbm, dpick_hbm, sel_hbm, d_tokens, gg, gu, gd,
                  fin, dpick, sel, rows, out_g, out_u, out_d, loaded, sems):
    loads = [pltpu.make_async_copy(sel_hbm, sel, loaded.at[4]),
             pltpu.make_async_copy(dpick_hbm, dpick, loaded.at[5])]
    parts = [pltpu.make_async_copy(fin_hbm.at[:, i], fin.at[:, i], loaded.at[i]) for i in range(4)]
    for copy in loads + [parts[i] for i in (3, 0, 1, 2)]:
        copy.start()
    copies = []

    def put(src, dst):
        copy = pltpu.make_async_copy(src, dst, sems.at[len(copies)])
        copy.start()
        copies.append(copy)

    for copy in loads:
        copy.wait()
    for k in range(4):
        at = pl.ds(k * 128, 128)
        rows[at] = dot(sel[:, at], dpick[...], ((0,), (0,))).astype(BF)
        put(rows.at[at], d_tokens.at[at])
    lane = iota((ROWS, 128), 1)
    parts[3].wait()
    rest = [fin[f, 3].astype(F32) for f in range(8)]
    for part, (out, dst) in enumerate(((out_g, gg), (out_u, gu), (out_d, gd))):
        parts[part].wait()
        for f in range(8):
            out[:, f * 128:(f + 1) * 128] = fin[f, part].astype(F32)
        for half in range(2):
            total = jnp.zeros((ROWS, 128), F32)
            for k in range(4):
                shift = ((k - part) * 32) % 128
                tile = rest[4 * half + k]
                tile = pltpu.roll(tile, shift, 1) if shift else tile
                total = jnp.where(lane // 32 == k, tile, total)
            out[:, 1024 + half * 128:1152 + half * 128] = total
        put(out, dst)
    for copy in copies:
        copy.wait()


def call(kernel, name, ins, outs, scratch=(), collective=None, flops=0):
    extra = {} if collective is None else dict(collective_id=collective, has_side_effects=True)
    vmem, any_ = pl.BlockSpec(memory_space=pltpu.VMEM), pl.BlockSpec(memory_space=pl.ANY)
    return pl.pallas_call(
        kernel,
        name=name,
        out_shape=[jax.ShapeDtypeStruct(shape, dtype) for shape, dtype, _ in outs],
        in_specs=[vmem if inside else any_ for inside in ins],
        out_specs=[vmem if inside else any_ for _, _, inside in outs],
        scratch_shapes=list(scratch),
        cost_estimate=pl.CostEstimate(flops=flops, bytes_accessed=8_000_000, transcendentals=0),
        compiler_params=pltpu.CompilerParams(vmem_limit_bytes=VMEM_LIMIT, **extra),
    )


def body(tokens, routes, gate_codes, cotangent, w_gate, w_up, w_down):
    dma = lambda n: pltpu.SemaphoreType.DMA((n,))
    buf = lambda *shape: pltpu.VMEM(shape, BF)
    quarter = buf(2, 2, ROWS, 128)
    half = buf(4, 2, ROWS, 128)
    fin, dpick, sel = call(
        expert_kernel, "expert", (1, 1, 0, 0, 0, 0, 0),
        [((4, 2, 4, ROWS, 128), BF, 0), ((CAP, D), BF, 0), ((CAP, TOK), BF, 0)],
        [buf(4, 2, 4, ROWS, 128), buf(CAP, D), buf(CAP, TOK), buf(TOK, D), buf(TOK, D), buf(3, ROWS, 128),
         buf(2, 8, CAP, D), buf(4, 8, ROWS, 128), pltpu.VMEM((4, D, 128), F32), buf(4, 2, 4, ROWS, 128),
         buf(8 * CAP, 384), buf(4, 2, CAP, D), buf(4, CAP, D), buf(3, CAP, D), buf(3, CAP, D),
         quarter, quarter, quarter, quarter, half, half, half, half, buf(7, ROWS, 128),
         buf(7, 4, ROWS, 128), buf(4, ROWS, 128), buf(3, ROWS, 128),
         dma(10 + NC), dma(15), dma(15), dma(14), dma(14), dma(13 * NC), dma(13 * NC), dma(4), dma(4),
         dma(19 * NC), dma(19 * NC),
         pltpu.SemaphoreType.REGULAR((3,))],
        collective=0, flops=4_000_000_000,
    )(routes.T, gate_codes.T, tokens, cotangent, w_gate, w_up, w_down)
    wide = pltpu.VMEM((ROWS, FF), F32)
    return tuple(call(
        finish_kernel, "finish", (0, 0, 0),
        [((TOK, D), BF, 0), ((ROWS, FF), F32, 0), ((ROWS, FF), F32, 0), ((ROWS, FF), F32, 0)],
        [buf(8, 4, ROWS, 128), buf(CAP, D), buf(CAP, TOK), buf(TOK, D), wide, wide, wide, dma(6), dma(7)], flops=200_000_000,
    )(fin.reshape(8, 4, ROWS, 128), dpick, sel))


def solution(mesh):
    both, dom = P(("rep", "dom"), None), P("dom", None)
    return jax.shard_map(
        body,
        mesh=mesh,
        in_specs=(both, both, both, both, dom, dom, dom),
        out_specs=(both, dom, dom, dom),
        check_vma=False,
    )
```

```python
import jax
import jax.numpy as jnp
from jax import lax
from jax.experimental import pallas as pl
from jax.experimental.pallas import tpu as pltpu
from jax.sharding import PartitionSpec as P

D, FF, CAP, TOK = 1792, 1280, 96, 512
ROWS = 224
HALF = CAP // 2
MESH = pl.DeviceIdType.MESH
BF, F32 = jnp.bfloat16, jnp.float32
VMEM_LIMIT = 56 * 1024 * 1024
CHUNKS = (
    (0, 48, "z", "steps"),
    (48, 48, "relay", "steps"),
    (96, 64, "relay", "steps"),
    (160, 32, "relay", "steps"),
    (192, 32, "relay", "once"),
)
NC = len(CHUNKS)
PLAN = (
    ("z_first", 0), ("opp", 1), ("near", 1), ("opp", 2), ("d_cores", 0), ("add", 1), ("near", 2), ("opp", 3),
    ("d_chips", 0), ("add", 2), ("near", 3), ("opp", 4), ("sum_y", 1), ("add", 3), ("near", 4), ("sum_y", 2),
    ("add", 4), ("z_sum", 0), ("sum_y", 3), ("sum_z", 1), ("sum_y", 4), ("y_sum", 0), ("sum_z", 2),
    ("sum_z", 3), ("onto_x", 1), ("sum_z", 4), ("onto_x", 0), ("d_sum", 0), ("onto_x", 2), ("onto_x", 3),
    ("onto_core", 1), ("leave", 1), ("onto_core", 0), ("onto_x", 4), ("onto_core", 4), ("leave", 0),
    ("onto_core", 2), ("leave", 4), ("onto_core", 3), ("leave", 2), ("leave", 3),
)

POS = {0: 0, 1: 1, 3: 2, 2: 3}


def coords():
    r, d = lax.axis_index("rep"), lax.axis_index("dom")
    return r // 8, (r // 2) % 4, r % 2, d // 4, d % 4


def dev(x, zh, c, zl, y):
    return (x * 8 + zh * 2 + c, zl * 4 + y)


def dot(a, b, dims=((1,), (0,))):
    return lax.dot_general(a, b, (dims, ((), ())), preferred_element_type=F32)


def iota(shape, axis):
    return lax.broadcasted_iota(jnp.int32, shape, axis)


def swiglu_back(g, u, dh):
    sig = 1.0 / (1.0 + jnp.exp(-g))
    act = g * sig
    return dh * u * sig * (1.0 + g * (1.0 - sig)), dh * act, act * u


def rows_of(xa, kind, lo, hi):
    return xa[kind, lo:hi].reshape((hi - lo) * CAP, D)


def forward_picked(lo, hi, xa, wa):
    part = lambda i: wa[i].reshape(D, 128)
    picked = rows_of(xa, 0, lo, hi)
    return dot(picked, jnp.concatenate([part(0), part(1)], axis=1)), dot(picked, part(3))


def forward_scaled(lo, hi, xa, wa, pre, rest, back):
    n = (hi - lo) * CAP
    part = lambda i: wa[i].reshape(D, 128)
    down = dot(rows_of(xa, 1, lo, hi), jnp.concatenate([part(2), part(3)], axis=1))
    lane = iota((n, 128), 1)
    rest = jnp.where(lane < 64, rest, down[:, 128:])
    dg, du, hid = swiglu_back(pre[:, :128], pre[:, 128:], down[:, :128])
    dg_r, du_r, hid_r = swiglu_back(rest, pltpu.roll(rest, 96, 1), pltpu.roll(rest, 64, 1))
    mix = jnp.where(lane < 32, dg_r, pltpu.roll(du_r, 32, 1))
    rest_p = jnp.where(lane < 64, mix, 0.0).astype(BF)
    rest_s = jnp.where((lane >= 64) & (lane < 96), pltpu.roll(hid_r, 64, 1), 0.0).astype(BF)
    up = jnp.concatenate([dg, du], axis=1).astype(BF)
    low = jnp.concatenate([hid.astype(BF), rest_s], axis=1)
    back[lo * CAP:hi * CAP, :256] = up
    back[lo * CAP:hi * CAP, 256:] = rest_p
    return up, low, rest_p


def terms_of(lo, hi, xa, at, up, low, rest_p):
    n = (hi - lo) * CAP
    first = ((0,), (0,))
    p_k = xa[0, lo:hi, :, pl.ds(at, 256)].reshape(n, 256)
    s_k = xa[1, lo:hi, :, pl.ds(at, 256)].reshape(n, 256)
    gu, hr, rr = dot(p_k, up, first), dot(s_k, low, first), dot(p_k, rest_p, first)
    return gu[:, :128], gu[:, 128:], hr[:, :128], hr[:, 128:] + rr


def expert_kernel(
    routes, codes, tok_hbm, cot_hbm, wg, wu, wd, fin_hbm, dpick_hbm, sel_hbm,
    fin, dpick, sel_own, tok, cot, tail, xa, wa, grad, gb, back, dp, dr, ds, df, ra, rb, ta, tb, low, mid, high, zs, zr, zw, zy, yr,
    local, ts, tr, ws, wr, gs, gr, es, er, ns, nr, told,
):
    x, zh, c, zl, y = coords()
    z, f = zh * 2 + zl, 2 * x + c
    sib = dev(x, zh, 1 - c, zl, y)
    ring = [dev((x + k) % 4, zh, c, zl, y) for k in (1, 2, 3)]
    right, left = ring[0], ring[2]
    yn, ys = (y + 1) % 4, (y + 3) % 4
    north, south = dev(x, zh, c, zl, yn), dev(x, zh, c, zl, ys)
    column = [dev(x, ((z + k) % 8) // 2, c, ((z + k) % 8) % 2, y) for k in range(1, 8)]
    pair = dev(x, zh, c, 1 - zl, y)
    nearby = [right, left, north, south, column[0], column[6]]
    partners = [sib] + nearby

    barrier = pltpu.get_barrier_semaphore()
    for partner in partners:
        pl.semaphore_signal(barrier, inc=1, device_id=partner, device_id_type=MESH)

    dom, dom_z = zl * 4 + y, (1 - zl) * 4 + y
    tile = pl.multiple_of(f * 128, 128)
    last = pl.multiple_of(1024 + (f // 4) * 128, 128)
    loads = [
        pltpu.make_async_copy(tok_hbm, tok, local.at[0]),
        pltpu.make_async_copy(cot_hbm, cot, local.at[1]),
    ]
    for i, w in enumerate((wg, wu, wd)):
        loads.append(pltpu.make_async_copy(w.at[:, pl.ds(tile, 128)], wa.at[i, dom], local.at[2 + i]))
        loads.append(pltpu.make_async_copy(w.at[:, pl.ds(last, 128)], tail.at[i], local.at[5 + i]))
    for copy in loads:
        copy.start()

    sends, outs = [], []

    def out(src, dst):
        copy = pltpu.make_async_copy(src, dst, local.at[8 + len(outs)])
        copy.start()
        outs.append(copy)

    def send(sems, index, src, dst, device):
        copy = pltpu.make_async_remote_copy(
            src_ref=src, dst_ref=dst, send_sem=sems[0].at[index], recv_sem=sems[1].at[index],
            device_id=device, device_id_type=MESH,
        )
        copy.start()
        sends.append(copy)
        return copy

    T, W, G, E, N = (ts, tr), (ws, wr), (gs, gr), (es, er), (ns, nr)
    slot = lambda delta, other: 2 * POS[delta] + other

    member = routes[...] == 0
    routed = jnp.max(jnp.where(member, 1.0, 0.0), axis=0, keepdims=True)
    code = jnp.sum(jnp.where(member, codes[...], 0), axis=0, keepdims=True).astype(F32)
    before = jnp.where(iota((TOK, TOK), 0) < iota((TOK, TOK), 1), 1.0, 0.0).astype(BF)
    rank = dot(jnp.broadcast_to(routed, (16, TOK)).astype(BF), before)[:1]
    hit = (jnp.broadcast_to(rank, (CAP, TOK)) == iota((CAP, TOK), 0).astype(F32)) & (
        jnp.broadcast_to(routed, (CAP, TOK)) > 0.0)
    sel = jnp.where(hit, 1.0, 0.0)
    weight = jnp.sum(sel * code, axis=1, keepdims=True) * (1.0 / 256.0)
    sel = sel.astype(BF)
    sel_own[...] = sel
    out(sel_own, sel_hbm)
    loads[0].wait()
    xa[0, 0] = dot(sel, tok[...]).astype(BF)
    def weights(index, half, dom_y, device):
        block = wa.at[2 * half:2 * half + 2, dom_y]
        return send(W, index, block, block, device)

    def around(index, kind, lo, to_right):
        to, device = (slot(3, 0), right) if to_right else (slot(1, 0), left)
        return send(T, index, xa.at[kind, 0, lo:lo + HALF], xa.at[kind, to, lo:lo + HALF], device)

    def onward(index, kind, delta):
        lo, device = (0, right) if delta == 3 else (HALF, left)
        return send(T, index, xa.at[kind, slot(delta, 0), lo:lo + HALF],
                    xa.at[kind, slot(2, 0), lo:lo + HALF], device)

    def share(index, kind, delta):
        return send(T, index, xa.at[kind, slot(delta, 0)], xa.at[kind, slot(delta, 1)], sib)

    def tell(index, devices):
        for device in devices:
            pl.semaphore_signal(told.at[index], inc=1, device_id=device, device_id_type=MESH)

    here, there = zl * 4, (1 - zl) * 4
    pl.semaphore_wait(barrier, len(partners))
    p_right, p_left = around(0, 0, 0, True), around(1, 0, HALF, False)
    p_right_2, p_left_2 = around(15, 0, HALF, True), around(16, 0, 0, False)
    for copy in loads[2:]:
        copy.wait()
    rest = jnp.zeros((ROWS, 128), F32)
    src, dst = iota((128, 128), 0), iota((128, 128), 1)
    for part in range(3):
        move = (src - (f % 4) * 32 == dst - part * 32) & (dst // 32 == part)
        rest += dot(tail[part], jnp.where(move, 1.0, 0.0).astype(BF))
    wa[3, dom] = rest.astype(BF)
    north_0, south_1 = weights(0, 0, dom, north), weights(1, 1, dom, south)
    pair_0, pair_1 = weights(2, 0, dom, pair), weights(3, 1, dom, pair)
    north_1, south_0 = weights(4, 1, dom, north), weights(5, 0, dom, south)
    loads[1].wait()
    xa[1, 0] = (weight * dot(sel, cot[...])).astype(BF)
    s_right, s_left = around(2, 1, 0, True), around(3, 1, HALF, False)
    s_right_2, s_left_2 = around(17, 1, HALF, True), around(18, 1, 0, False)
    x_sib = send(T, 4, xa.at[:, 0], xa.at[:, slot(0, 1)], sib)

    tell(0, nearby)
    north_0.wait_recv()
    all_w = [weights(6, 0, here + ys, north)]
    south_1.wait_recv()
    all_w.append(weights(7, 1, here + yn, south))
    pair_0.wait_recv()
    z_north_0 = weights(8, 0, dom_z, north)
    pair_1.wait_recv()
    z_south_1 = weights(9, 1, dom_z, south)
    all_w += [weights(10, 1, dom_z, north), weights(11, 0, dom_z, south), north_1, south_0]
    pl.semaphore_wait(told.at[0], len(nearby))
    tell(1, (column[0], column[6]))
    p_right.wait_recv()
    p_on_r = onward(5, 0, 3)
    p_left.wait_recv()
    p_on_l = onward(6, 0, 1)
    p_right_2.wait_recv()
    p_left_2.wait_recv()
    share_p3, share_p1 = share(9, 0, 3), share(10, 0, 1)
    z_north_0.wait_recv()
    all_w.append(weights(12, 0, there + ys, north))
    z_south_1.wait_recv()
    all_w.append(weights(13, 1, there + yn, south))
    pl.semaphore_wait(told.at[1], 2)
    tell(2, (column[0], column[6]))
    s_right.wait_recv()
    s_on_r = onward(7, 1, 3)
    s_left.wait_recv()
    s_on_l = onward(8, 1, 1)
    s_right_2.wait_recv()
    s_left_2.wait_recv()
    share_s3, share_s1 = share(11, 1, 3), share(12, 1, 1)
    pl.semaphore_wait(told.at[2], 2)
    for copy in all_w + [x_sib, share_p3, share_p1, share_s3, share_s1]:
        copy.wait_recv()

    up6 = forward_scaled(0, 6, xa, wa, *forward_picked(0, 6, xa, wa), back)
    p_on_r.wait_recv()
    p_on_l.wait_recv()
    share_p2 = share(13, 0, 2)

    def columns(k, carry):
        at = pl.multiple_of(k * 256, 256)
        for i, term in enumerate(terms_of(0, 6, xa, at, *up6)):
            grad[i, pl.ds(at, 256), :] = term
        return carry

    lax.fori_loop(0, D // 256, columns, 0)
    s_on_r.wait_recv()
    s_on_l.wait_recv()
    share_s2 = share(14, 1, 2)
    share_p2.wait_recv()
    pre = forward_picked(6, 8, xa, wa)
    share_s2.wait_recv()
    up2 = forward_scaled(6, 8, xa, wa, *pre, back)
    for k in range(D // 256):
        lo = k * 256
        for i, term in enumerate(terms_of(6, 8, xa, lo, *up2)):
            total = (grad[i, lo:lo + 256, :] + term).astype(BF)
            at = lo
            while at < lo + 256:
                d, r = at // ROWS, at % ROWS
                n = min(ROWS - r, lo + 256 - at)
                gb[i, d // 4, d % 4, r:r + n, :] = total[at - lo:at - lo + n]
                at += n

    f32 = lambda ref: ref.astype(F32)
    opposite = (y + 2) % 4
    ways = [dev(x, zh, c, zl, (y + k) % 4) for k in (1, 2, 3)]
    got = {}

    def rows(s):
        return pl.ds(CHUNKS[s][0], CHUNKS[s][1])

    def opp(s):
        r = rows(s)
        got[s, "opp"] = (send(G, 13 * s, gb.at[0:2, :, opposite, r], ra.at[:, :, r], north),
                         send(G, 13 * s + 1, gb.at[2:4, :, opposite, r], rb.at[:, :, r], south))

    def near(s):
        r = rows(s)
        got[s, "y"] = [send(G, 13 * s + 2, gb.at[2:4, :, yn, r], low.at[2:4, :, r], north),
                       send(G, 13 * s + 3, gb.at[0:2, :, ys, r], high.at[0:2, :, r], south)]

    def add(s):
        r = rows(s)
        got[s, "opp"][0].wait_recv()
        ta[:, :, r] = (f32(ra[:, :, r]) + f32(gb[0:2, :, yn, r])).astype(BF)
        got[s, "y"].append(send(G, 13 * s + 4, ta.at[:, :, r], low.at[0:2, :, r], north))
        got[s, "opp"][1].wait_recv()
        tb[:, :, r] = (f32(rb[:, :, r]) + f32(gb[2:4, :, ys, r])).astype(BF)
        got[s, "y"].append(send(G, 13 * s + 5, tb.at[:, :, r], high.at[2:4, :, r], south))

    def straight(s):
        r = rows(s)
        got[s, "y"] = [send(G, 13 * s + k, gb.at[:, :, (y + k) % 4, r], to.at[:, :, r], ways[k - 1])
                       for k, to in ((2, mid), (1, low), (3, high))]

    def sum_y(s):
        r = rows(s)
        for copy in got[s, "y"]:
            copy.wait_recv()
        total = f32(gb[:, :, y, r]) + f32(low[:, :, r]) + f32(high[:, :, r])
        if CHUNKS[s][2] == "direct":
            total += f32(mid[:, :, r])
        zs[:, :, r] = total.astype(BF)
        got[s, "z"] = []
        for k in (4, 3, 5, 2, 6, 1, 7):
            to = (z + k) % 8
            got[s, "z"].append(send(G, 13 * s + 5 + k, zs.at[to // 2, to % 2, r], zr.at[k - 1, r],
                                    column[k - 1]))

    def sum_z(s):
        r = rows(s)
        for copy in got[s, "z"]:
            copy.wait_recv()
        total = f32(zs[zh, zl, r])
        for k in range(7):
            total += f32(zr[k, r])
        fin[x, c, zh, r] = total.astype(BF)
        spread(s)

    def z_first(s):
        r = rows(s)
        got[s, "z"] = []
        for k in (4, 3, 5, 2, 6, 1, 7):
            to = (z + k) % 8
            got[s, "z"].append(send(G, 13 * s + 5 + k, gb.at[to // 2, to % 2, :, r], zw.at[k - 1, :, r],
                                    column[k - 1]))

    def z_sum(s):
        r = rows(s)
        for copy in got[s, "z"]:
            copy.wait_recv()
        total = f32(gb[zh, zl, :, r])
        for k in range(7):
            total += f32(zw[k, :, r])
        zy[:, r] = total.astype(BF)
        got[s, "y"] = [send(G, 13 * s + k, zy.at[(y + k) % 4, r], yr.at[k - 1, r], ways[k - 1])
                       for k in (2, 1, 3)]

    def y_sum(s):
        r = rows(s)
        for copy in got[s, "y"]:
            copy.wait_recv()
        fin[x, c, zh, r] = (f32(zy[y, r]) + f32(yr[0, r]) + f32(yr[1, r]) + f32(yr[2, r])).astype(BF)
        spread(s)

    def spread(s):
        piece = fin.at[x, c, zh, rows(s)]
        if CHUNKS[s][3] == "steps":
            got[s, "zh"] = [send(N, 19 * s + k - 1, piece, piece, dev(x, (zh + k) % 4, c, zl, y))
                            for k in (1, 2, 3)]
            got[s, "x"] = {(j, 0): send(N, 19 * s + 2 + j, piece, piece, ring[j - 1]) for j in (2, 1, 3)}
        else:
            got[s, "x"] = {}
            for j, k in ((2, 2), (1, 2), (3, 2), (2, 1), (2, 3), (0, 2), (1, 1), (1, 3), (3, 1), (3, 3),
                         (2, 0), (0, 1), (0, 3), (1, 0), (3, 0)):
                got[s, "x"][j, k] = send(N, 19 * s + 4 * k + j - 1, piece, piece,
                                         dev((x + j) % 4, (zh + k) % 4, c, zl, y))

    def onto_x(s):
        if CHUNKS[s][3] == "steps":
            for k in (1, 3, 2):
                got[s, "zh"][k - 1].wait_recv()
                piece = fin.at[x, c, (zh + 4 - k) % 4, rows(s)]
                for j in (2, 1, 3):
                    got[s, "x"][j, k] = send(N, 19 * s + 2 + 3 * k + j, piece, piece, ring[j - 1])
        else:
            for k in (1, 3, 2):
                got[s, "x"][0, k].wait_recv()
        block = fin.at[x, c, :, rows(s)]
        got[s, "core"] = [send(N, 19 * s + 15, block, block, sib)]

    def onto_core(s):
        for j in (1, 3, 2):
            for k in range(4):
                got[s, "x"][j, k].wait_recv()
            block = fin.at[(x + 4 - j) % 4, c, :, rows(s)]
            got[s, "core"].append(send(N, 19 * s + 15 + j, block, block, sib))

    def d_cores(_):
        for k in range(D // 256):
            flat = jnp.concatenate(
                [wa.at[i].reshape(D, 128)[k * 256:(k + 1) * 256] for i in (0, 1, 3)], axis=1)
            out = dot(back[...], flat, ((1,), (1,))).astype(BF)
            dp[:, :, :, k * 256:(k + 1) * 256] = out.reshape(4, 2, CAP, 256)
        got["d"] = send(E, 0, dp.at[:, 1], dr, sib)

    def d_chips(_):
        got["d"].wait_recv()
        for k in (2, 1, 3):
            ds[k - 1] = (f32(dr[POS[k]]) + f32(dp[POS[k], 0])).astype(BF)
            got["d", k] = send(E, k, ds.at[k - 1], df.at[k - 1], ring[k - 1])

    def d_sum(_):
        for k in (1, 2, 3):
            got["d", k].wait_recv()
        total = f32(dr[0]) + f32(dp[0, 0]) + f32(df[0]) + f32(df[1]) + f32(df[2])
        dpick[...] = total.astype(BF)
        out(dpick, dpick_hbm)

    def leave(s):
        for copy in got[s, "core"]:
            copy.wait_recv()
        out(fin.at[:, :, :, rows(s)], fin_hbm.at[:, :, :, rows(s)])

    for stage, s in PLAN:
        dict(opp=opp, near=near, add=add, straight=straight, sum_y=sum_y, sum_z=sum_z, z_first=z_first,
             z_sum=z_sum, y_sum=y_sum, onto_x=onto_x, onto_core=onto_core, d_cores=d_cores,
             d_chips=d_chips, d_sum=d_sum, leave=leave)[stage](s)

    for copy in sends:
        copy.wait_send()
    for copy in outs:
        copy.wait()


def finish_kernel(fin_hbm, dpick_hbm, sel_hbm, d_tokens, gg, gu, gd,
                  fin, dpick, sel, rows, out_g, out_u, out_d, loaded, sems):
    loads = [pltpu.make_async_copy(sel_hbm, sel, loaded.at[4]),
             pltpu.make_async_copy(dpick_hbm, dpick, loaded.at[5])]
    parts = [pltpu.make_async_copy(fin_hbm.at[:, i], fin.at[:, i], loaded.at[i]) for i in range(4)]
    for copy in loads + [parts[i] for i in (3, 0, 1, 2)]:
        copy.start()
    copies = []

    def put(src, dst):
        copy = pltpu.make_async_copy(src, dst, sems.at[len(copies)])
        copy.start()
        copies.append(copy)

    for copy in loads:
        copy.wait()
    for k in range(4):
        at = pl.ds(k * 128, 128)
        rows[at] = dot(sel[:, at], dpick[...], ((0,), (0,))).astype(BF)
        put(rows.at[at], d_tokens.at[at])
    lane = iota((ROWS, 128), 1)
    parts[3].wait()
    rest = [fin[f, 3].astype(F32) for f in range(8)]
    for part, (out, dst) in enumerate(((out_g, gg), (out_u, gu), (out_d, gd))):
        parts[part].wait()
        for f in range(8):
            out[:, f * 128:(f + 1) * 128] = fin[f, part].astype(F32)
        for half in range(2):
            total = jnp.zeros((ROWS, 128), F32)
            for k in range(4):
                shift = ((k - part) * 32) % 128
                tile = rest[4 * half + k]
                tile = pltpu.roll(tile, shift, 1) if shift else tile
                total = jnp.where(lane // 32 == k, tile, total)
            out[:, 1024 + half * 128:1152 + half * 128] = total
        put(out, dst)
    for copy in copies:
        copy.wait()


def call(kernel, name, ins, outs, scratch=(), collective=None, flops=0):
    extra = {} if collective is None else dict(collective_id=collective, has_side_effects=True)
    vmem, any_ = pl.BlockSpec(memory_space=pltpu.VMEM), pl.BlockSpec(memory_space=pl.ANY)
    return pl.pallas_call(
        kernel,
        name=name,
        out_shape=[jax.ShapeDtypeStruct(shape, dtype) for shape, dtype, _ in outs],
        in_specs=[vmem if inside else any_ for inside in ins],
        out_specs=[vmem if inside else any_ for _, _, inside in outs],
        scratch_shapes=list(scratch),
        cost_estimate=pl.CostEstimate(flops=flops, bytes_accessed=8_000_000, transcendentals=0),
        compiler_params=pltpu.CompilerParams(vmem_limit_bytes=VMEM_LIMIT, **extra),
    )


def body(tokens, routes, gate_codes, cotangent, w_gate, w_up, w_down):
    dma = lambda n: pltpu.SemaphoreType.DMA((n,))
    buf = lambda *shape: pltpu.VMEM(shape, BF)
    quarter = buf(2, 2, ROWS, 128)
    half = buf(4, 2, ROWS, 128)
    fin, dpick, sel = call(
        expert_kernel, "expert", (1, 1, 0, 0, 0, 0, 0),
        [((4, 2, 4, ROWS, 128), BF, 0), ((CAP, D), BF, 0), ((CAP, TOK), BF, 0)],
        [buf(4, 2, 4, ROWS, 128), buf(CAP, D), buf(CAP, TOK), buf(TOK, D), buf(TOK, D), buf(3, ROWS, 128),
         buf(2, 8, CAP, D), buf(4, 8, ROWS, 128), pltpu.VMEM((4, D, 128), F32), buf(4, 2, 4, ROWS, 128),
         buf(8 * CAP, 384), buf(4, 2, CAP, D), buf(4, CAP, D), buf(3, CAP, D), buf(3, CAP, D),
         quarter, quarter, quarter, quarter, half, half, half, half, buf(7, ROWS, 128),
         buf(7, 4, ROWS, 128), buf(4, ROWS, 128), buf(3, ROWS, 128),
         dma(10 + NC), dma(19), dma(19), dma(14), dma(14), dma(13 * NC), dma(13 * NC), dma(4), dma(4),
         dma(19 * NC), dma(19 * NC),
         pltpu.SemaphoreType.REGULAR((3,))],
        collective=0, flops=4_000_000_000,
    )(routes.T, gate_codes.T, tokens, cotangent, w_gate, w_up, w_down)
    wide = pltpu.VMEM((ROWS, FF), F32)
    return tuple(call(
        finish_kernel, "finish", (0, 0, 0),
        [((TOK, D), BF, 0), ((ROWS, FF), F32, 0), ((ROWS, FF), F32, 0), ((ROWS, FF), F32, 0)],
        [buf(8, 4, ROWS, 128), buf(CAP, D), buf(CAP, TOK), buf(TOK, D), wide, wide, wide, dma(6), dma(7)], flops=200_000_000,
    )(fin.reshape(8, 4, ROWS, 128), dpick, sel))


def solution(mesh):
    both, dom = P(("rep", "dom"), None), P("dom", None)
    return jax.shard_map(
        body,
        mesh=mesh,
        in_specs=(both, both, both, both, dom, dom, dom),
        out_specs=(both, dom, dom, dom),
        check_vma=False,
    )
```

```python
import jax
import jax.numpy as jnp
from jax import lax
from jax.experimental import pallas as pl
from jax.experimental.pallas import tpu as pltpu
from jax.sharding import PartitionSpec as P

D, FF, CAP, TOK = 1792, 1280, 96, 512
ROWS = 224
HALF = CAP // 2
MESH = pl.DeviceIdType.MESH
BF, F32 = jnp.bfloat16, jnp.float32
VMEM_LIMIT = 56 * 1024 * 1024
CHUNKS = (
    (0, 48, "z", "steps"),
    (48, 48, "relay", "steps"),
    (96, 64, "relay", "steps"),
    (160, 32, "relay", "steps"),
    (192, 32, "relay", "once"),
)
NC = len(CHUNKS)
PLAN = (
    ("z_first", 0), ("opp", 1), ("near", 1), ("opp", 2), ("d_cores", 0), ("add", 1), ("near", 2), ("opp", 3),
    ("d_chips", 0), ("add", 2), ("near", 3), ("opp", 4), ("sum_y", 1), ("add", 3), ("near", 4), ("sum_y", 2),
    ("add", 4), ("z_sum", 0), ("sum_y", 3), ("sum_z", 1), ("sum_y", 4), ("y_sum", 0), ("sum_z", 2),
    ("sum_z", 3), ("onto_x", 1), ("sum_z", 4), ("onto_x", 0), ("d_sum", 0), ("onto_x", 2), ("onto_x", 3),
    ("onto_core", 1), ("leave", 1), ("onto_core", 0), ("onto_x", 4), ("onto_core", 4), ("leave", 0),
    ("onto_core", 2), ("leave", 4), ("onto_core", 3), ("leave", 2), ("leave", 3),
)

POS = {0: 0, 1: 1, 3: 2, 2: 3}


def coords():
    r, d = lax.axis_index("rep"), lax.axis_index("dom")
    return r // 8, (r // 2) % 4, r % 2, d // 4, d % 4


def dev(x, zh, c, zl, y):
    return (x * 8 + zh * 2 + c, zl * 4 + y)


def dot(a, b, dims=((1,), (0,))):
    return lax.dot_general(a, b, (dims, ((), ())), preferred_element_type=F32)


def iota(shape, axis):
    return lax.broadcasted_iota(jnp.int32, shape, axis)


def swiglu_back(g, u, dh):
    sig = 1.0 / (1.0 + jnp.exp(-g))
    act = g * sig
    return dh * u * sig * (1.0 + g * (1.0 - sig)), dh * act, act * u


def rows_of(xa, kind, lo, hi):
    return xa[kind, lo:hi].reshape((hi - lo) * CAP, D)


def forward_picked(lo, hi, xa, wa):
    part = lambda i: wa[i].reshape(D, 128)
    picked = rows_of(xa, 0, lo, hi)
    return dot(picked, jnp.concatenate([part(0), part(1)], axis=1)), dot(picked, part(3))


def forward_scaled(lo, hi, xa, wa, pre, rest, back):
    n = (hi - lo) * CAP
    part = lambda i: wa[i].reshape(D, 128)
    down = dot(rows_of(xa, 1, lo, hi), jnp.concatenate([part(2), part(3)], axis=1))
    lane = iota((n, 128), 1)
    rest = jnp.where(lane < 64, rest, down[:, 128:])
    dg, du, hid = swiglu_back(pre[:, :128], pre[:, 128:], down[:, :128])
    dg_r, du_r, hid_r = swiglu_back(rest, pltpu.roll(rest, 96, 1), pltpu.roll(rest, 64, 1))
    mix = jnp.where(lane < 32, dg_r, pltpu.roll(du_r, 32, 1))
    rest_p = jnp.where(lane < 64, mix, 0.0).astype(BF)
    rest_s = jnp.where((lane >= 64) & (lane < 96), pltpu.roll(hid_r, 64, 1), 0.0).astype(BF)
    up = jnp.concatenate([dg, du], axis=1).astype(BF)
    low = jnp.concatenate([hid.astype(BF), rest_s], axis=1)
    back[lo * CAP:hi * CAP, :256] = up
    back[lo * CAP:hi * CAP, 256:] = rest_p
    return up, low, rest_p


def terms_of(lo, hi, xa, at, up, low, rest_p):
    n = (hi - lo) * CAP
    first = ((0,), (0,))
    p_k = xa[0, lo:hi, :, pl.ds(at, 256)].reshape(n, 256)
    s_k = xa[1, lo:hi, :, pl.ds(at, 256)].reshape(n, 256)
    gu, hr, rr = dot(p_k, up, first), dot(s_k, low, first), dot(p_k, rest_p, first)
    return gu[:, :128], gu[:, 128:], hr[:, :128], hr[:, 128:] + rr


def expert_kernel(
    routes, codes, tok_hbm, cot_hbm, wg, wu, wd, fin_hbm, dpick_hbm, sel_hbm,
    fin, dpick, sel_own, tok, cot, tail, xa, wa, grad, gb, back, dp, dr, ds, df, ra, rb, ta, tb, low, mid, high, zs, zr, zw, zy, yr,
    local, ts, tr, ws, wr, gs, gr, es, er, ns, nr, told,
):
    x, zh, c, zl, y = coords()
    z, f = zh * 2 + zl, 2 * x + c
    sib = dev(x, zh, 1 - c, zl, y)
    ring = [dev((x + k) % 4, zh, c, zl, y) for k in (1, 2, 3)]
    right, left = ring[0], ring[2]
    yn, ys = (y + 1) % 4, (y + 3) % 4
    north, south = dev(x, zh, c, zl, yn), dev(x, zh, c, zl, ys)
    column = [dev(x, ((z + k) % 8) // 2, c, ((z + k) % 8) % 2, y) for k in range(1, 8)]
    pair = dev(x, zh, c, 1 - zl, y)
    nearby = [right, left, north, south, column[0], column[6]]
    partners = [sib] + nearby

    barrier = pltpu.get_barrier_semaphore()
    for partner in partners:
        pl.semaphore_signal(barrier, inc=1, device_id=partner, device_id_type=MESH)

    dom, dom_z = zl * 4 + y, (1 - zl) * 4 + y
    tile = pl.multiple_of(f * 128, 128)
    last = pl.multiple_of(1024 + (f // 4) * 128, 128)
    loads = [
        pltpu.make_async_copy(tok_hbm, tok, local.at[0]),
        pltpu.make_async_copy(cot_hbm, cot, local.at[1]),
    ]
    for i, w in enumerate((wg, wu, wd)):
        loads.append(pltpu.make_async_copy(w.at[:, pl.ds(tile, 128)], wa.at[i, dom], local.at[2 + i]))
        loads.append(pltpu.make_async_copy(w.at[:, pl.ds(last, 128)], tail.at[i], local.at[5 + i]))
    for copy in loads:
        copy.start()

    sends, outs = [], []

    def out(src, dst):
        copy = pltpu.make_async_copy(src, dst, local.at[8 + len(outs)])
        copy.start()
        outs.append(copy)

    def send(sems, index, src, dst, device):
        copy = pltpu.make_async_remote_copy(
            src_ref=src, dst_ref=dst, send_sem=sems[0].at[index], recv_sem=sems[1].at[index],
            device_id=device, device_id_type=MESH,
        )
        copy.start()
        sends.append(copy)
        return copy

    T, W, G, E, N = (ts, tr), (ws, wr), (gs, gr), (es, er), (ns, nr)
    slot = lambda delta, other: 2 * POS[delta] + other

    member = routes[...] == 0
    routed = jnp.max(jnp.where(member, 1.0, 0.0), axis=0, keepdims=True)
    code = jnp.sum(jnp.where(member, codes[...], 0), axis=0, keepdims=True).astype(F32)
    before = jnp.where(iota((TOK, TOK), 0) < iota((TOK, TOK), 1), 1.0, 0.0).astype(BF)
    rank = dot(jnp.broadcast_to(routed, (16, TOK)).astype(BF), before)[:1]
    hit = (jnp.broadcast_to(rank, (CAP, TOK)) == iota((CAP, TOK), 0).astype(F32)) & (
        jnp.broadcast_to(routed, (CAP, TOK)) > 0.0)
    sel = jnp.where(hit, 1.0, 0.0)
    weight = jnp.sum(sel * code, axis=1, keepdims=True) * (1.0 / 256.0)
    sel = sel.astype(BF)
    sel_own[...] = sel
    out(sel_own, sel_hbm)
    loads[0].wait()
    xa[0, 0] = dot(sel, tok[...]).astype(BF)
    def weights(index, half, dom_y, device):
        block = wa.at[2 * half:2 * half + 2, dom_y]
        return send(W, index, block, block, device)

    def around(index, kind, lo, to_right):
        to, device = (slot(3, 0), right) if to_right else (slot(1, 0), left)
        return send(T, index, xa.at[kind, 0, lo:lo + HALF], xa.at[kind, to, lo:lo + HALF], device)

    def onward(index, kind, delta):
        lo, device = (0, right) if delta == 3 else (HALF, left)
        return send(T, index, xa.at[kind, slot(delta, 0), lo:lo + HALF],
                    xa.at[kind, slot(2, 0), lo:lo + HALF], device)

    def share(index, kind, delta):
        return send(T, index, xa.at[kind, slot(delta, 0)], xa.at[kind, slot(delta, 1)], sib)

    def tell(index, devices):
        for device in devices:
            pl.semaphore_signal(told.at[index], inc=1, device_id=device, device_id_type=MESH)

    here, there = zl * 4, (1 - zl) * 4
    pl.semaphore_wait(barrier, len(partners))
    p_right, p_left = around(0, 0, 0, True), around(1, 0, HALF, False)
    p_right_2, p_left_2 = around(15, 0, HALF, True), around(16, 0, 0, False)
    for copy in loads[2:]:
        copy.wait()
    rest = jnp.zeros((ROWS, 128), F32)
    src, dst = iota((128, 128), 0), iota((128, 128), 1)
    for part in range(3):
        move = (src - (f % 4) * 32 == dst - part * 32) & (dst // 32 == part)
        rest += dot(tail[part], jnp.where(move, 1.0, 0.0).astype(BF))
    wa[3, dom] = rest.astype(BF)
    north_0, south_1 = weights(0, 0, dom, north), weights(1, 1, dom, south)
    pair_0, pair_1 = weights(2, 0, dom, pair), weights(3, 1, dom, pair)
    north_1, south_0 = weights(4, 1, dom, north), weights(5, 0, dom, south)
    loads[1].wait()
    xa[1, 0] = (weight * dot(sel, cot[...])).astype(BF)
    s_right, s_left = around(2, 1, 0, True), around(3, 1, HALF, False)
    s_right_2, s_left_2 = around(17, 1, HALF, True), around(18, 1, 0, False)
    x_sib = send(T, 4, xa.at[:, 0], xa.at[:, slot(0, 1)], sib)

    tell(0, nearby)
    north_0.wait_recv()
    all_w = [weights(6, 0, here + ys, north)]
    south_1.wait_recv()
    all_w.append(weights(7, 1, here + yn, south))
    pair_0.wait_recv()
    z_north_0 = weights(8, 0, dom_z, north)
    pair_1.wait_recv()
    z_south_1 = weights(9, 1, dom_z, south)
    all_w += [weights(10, 1, dom_z, north), weights(11, 0, dom_z, south), north_1, south_0]
    pl.semaphore_wait(told.at[0], len(nearby))
    tell(1, (column[0], column[6]))
    p_right.wait_recv()
    p_on_r = onward(5, 0, 3)
    p_left.wait_recv()
    p_on_l = onward(6, 0, 1)
    p_right_2.wait_recv()
    p_left_2.wait_recv()
    share_p3, share_p1 = share(9, 0, 3), share(10, 0, 1)
    z_north_0.wait_recv()
    all_w.append(weights(12, 0, there + ys, north))
    z_south_1.wait_recv()
    all_w.append(weights(13, 1, there + yn, south))
    pl.semaphore_wait(told.at[1], 2)
    tell(2, (column[0], column[6]))
    s_right.wait_recv()
    s_on_r = onward(7, 1, 3)
    s_left.wait_recv()
    s_on_l = onward(8, 1, 1)
    s_right_2.wait_recv()
    s_left_2.wait_recv()
    share_s3, share_s1 = share(11, 1, 3), share(12, 1, 1)
    pl.semaphore_wait(told.at[2], 2)
    for copy in all_w + [x_sib, share_p3, share_p1, share_s3, share_s1]:
        copy.wait_recv()

    up6 = forward_scaled(0, 6, xa, wa, *forward_picked(0, 6, xa, wa), back)
    p_on_r.wait_recv()
    p_on_l.wait_recv()
    share_p2 = share(13, 0, 2)

    def columns(k, carry):
        at = pl.multiple_of(k * 256, 256)
        for i, term in enumerate(terms_of(0, 6, xa, at, *up6)):
            grad[i, pl.ds(at, 256), :] = term
        return carry

    lax.fori_loop(0, D // 256, columns, 0)
    s_on_r.wait_recv()
    s_on_l.wait_recv()
    share_s2 = share(14, 1, 2)
    share_p2.wait_recv()
    pre = forward_picked(6, 8, xa, wa)

    def token_part(lo, hi):
        for k in range(D // 256):
            flat = jnp.concatenate(
                [wa.at[i].reshape(D, 128)[k * 256:(k + 1) * 256] for i in (0, 1, 3)], axis=1)
            part = dot(back[2 * lo * CAP:2 * hi * CAP], flat, ((1,), (1,))).astype(BF)
            dp[lo:hi, :, :, k * 256:(k + 1) * 256] = part.reshape(hi - lo, 2, CAP, 256)

    token_part(0, 1)
    share_s2.wait_recv()
    up2 = forward_scaled(6, 8, xa, wa, *pre, back)
    for k in range(D // 256):
        lo = k * 256
        for i, term in enumerate(terms_of(6, 8, xa, lo, *up2)):
            total = (grad[i, lo:lo + 256, :] + term).astype(BF)
            at = lo
            while at < lo + 256:
                d, r = at // ROWS, at % ROWS
                n = min(ROWS - r, lo + 256 - at)
                gb[i, d // 4, d % 4, r:r + n, :] = total[at - lo:at - lo + n]
                at += n

    f32 = lambda ref: ref.astype(F32)
    opposite = (y + 2) % 4
    ways = [dev(x, zh, c, zl, (y + k) % 4) for k in (1, 2, 3)]
    got = {}

    def rows(s):
        return pl.ds(CHUNKS[s][0], CHUNKS[s][1])

    def opp(s):
        r = rows(s)
        got[s, "opp"] = (send(G, 13 * s, gb.at[0:2, :, opposite, r], ra.at[:, :, r], north),
                         send(G, 13 * s + 1, gb.at[2:4, :, opposite, r], rb.at[:, :, r], south))

    def near(s):
        r = rows(s)
        got[s, "y"] = [send(G, 13 * s + 2, gb.at[2:4, :, yn, r], low.at[2:4, :, r], north),
                       send(G, 13 * s + 3, gb.at[0:2, :, ys, r], high.at[0:2, :, r], south)]

    def add(s):
        r = rows(s)
        got[s, "opp"][0].wait_recv()
        ta[:, :, r] = (f32(ra[:, :, r]) + f32(gb[0:2, :, yn, r])).astype(BF)
        got[s, "y"].append(send(G, 13 * s + 4, ta.at[:, :, r], low.at[0:2, :, r], north))
        got[s, "opp"][1].wait_recv()
        tb[:, :, r] = (f32(rb[:, :, r]) + f32(gb[2:4, :, ys, r])).astype(BF)
        got[s, "y"].append(send(G, 13 * s + 5, tb.at[:, :, r], high.at[2:4, :, r], south))

    def straight(s):
        r = rows(s)
        got[s, "y"] = [send(G, 13 * s + k, gb.at[:, :, (y + k) % 4, r], to.at[:, :, r], ways[k - 1])
                       for k, to in ((2, mid), (1, low), (3, high))]

    def sum_y(s):
        r = rows(s)
        for copy in got[s, "y"]:
            copy.wait_recv()
        total = f32(gb[:, :, y, r]) + f32(low[:, :, r]) + f32(high[:, :, r])
        if CHUNKS[s][2] == "direct":
            total += f32(mid[:, :, r])
        zs[:, :, r] = total.astype(BF)
        got[s, "z"] = []
        for k in (4, 3, 5, 2, 6, 1, 7):
            to = (z + k) % 8
            got[s, "z"].append(send(G, 13 * s + 5 + k, zs.at[to // 2, to % 2, r], zr.at[k - 1, r],
                                    column[k - 1]))

    def sum_z(s):
        r = rows(s)
        for copy in got[s, "z"]:
            copy.wait_recv()
        total = f32(zs[zh, zl, r])
        for k in range(7):
            total += f32(zr[k, r])
        fin[x, c, zh, r] = total.astype(BF)
        spread(s)

    def z_first(s):
        r = rows(s)
        got[s, "z"] = []
        for k in (4, 3, 5, 2, 6, 1, 7):
            to = (z + k) % 8
            got[s, "z"].append(send(G, 13 * s + 5 + k, gb.at[to // 2, to % 2, :, r], zw.at[k - 1, :, r],
                                    column[k - 1]))

    def z_sum(s):
        r = rows(s)
        for copy in got[s, "z"]:
            copy.wait_recv()
        total = f32(gb[zh, zl, :, r])
        for k in range(7):
            total += f32(zw[k, :, r])
        zy[:, r] = total.astype(BF)
        got[s, "y"] = [send(G, 13 * s + k, zy.at[(y + k) % 4, r], yr.at[k - 1, r], ways[k - 1])
                       for k in (2, 1, 3)]

    def y_sum(s):
        r = rows(s)
        for copy in got[s, "y"]:
            copy.wait_recv()
        fin[x, c, zh, r] = (f32(zy[y, r]) + f32(yr[0, r]) + f32(yr[1, r]) + f32(yr[2, r])).astype(BF)
        spread(s)

    def spread(s):
        piece = fin.at[x, c, zh, rows(s)]
        if CHUNKS[s][3] == "steps":
            got[s, "zh"] = [send(N, 19 * s + k - 1, piece, piece, dev(x, (zh + k) % 4, c, zl, y))
                            for k in (1, 2, 3)]
            got[s, "x"] = {(j, 0): send(N, 19 * s + 2 + j, piece, piece, ring[j - 1]) for j in (2, 1, 3)}
        else:
            got[s, "x"] = {}
            for j, k in ((2, 2), (1, 2), (3, 2), (2, 1), (2, 3), (0, 2), (1, 1), (1, 3), (3, 1), (3, 3),
                         (2, 0), (0, 1), (0, 3), (1, 0), (3, 0)):
                got[s, "x"][j, k] = send(N, 19 * s + 4 * k + j - 1, piece, piece,
                                         dev((x + j) % 4, (zh + k) % 4, c, zl, y))

    def onto_x(s):
        if CHUNKS[s][3] == "steps":
            for k in (1, 3, 2):
                got[s, "zh"][k - 1].wait_recv()
                piece = fin.at[x, c, (zh + 4 - k) % 4, rows(s)]
                for j in (2, 1, 3):
                    got[s, "x"][j, k] = send(N, 19 * s + 2 + 3 * k + j, piece, piece, ring[j - 1])
        else:
            for k in (1, 3, 2):
                got[s, "x"][0, k].wait_recv()
        block = fin.at[x, c, :, rows(s)]
        got[s, "core"] = [send(N, 19 * s + 15, block, block, sib)]

    def onto_core(s):
        for j in (1, 3, 2):
            for k in range(4):
                got[s, "x"][j, k].wait_recv()
            block = fin.at[(x + 4 - j) % 4, c, :, rows(s)]
            got[s, "core"].append(send(N, 19 * s + 15 + j, block, block, sib))

    def d_cores(_):
        token_part(1, 4)
        got["d"] = send(E, 0, dp.at[:, 1], dr, sib)

    def d_chips(_):
        got["d"].wait_recv()
        for k in (2, 1, 3):
            ds[k - 1] = (f32(dr[POS[k]]) + f32(dp[POS[k], 0])).astype(BF)
            got["d", k] = send(E, k, ds.at[k - 1], df.at[k - 1], ring[k - 1])

    def d_sum(_):
        for k in (1, 2, 3):
            got["d", k].wait_recv()
        total = f32(dr[0]) + f32(dp[0, 0]) + f32(df[0]) + f32(df[1]) + f32(df[2])
        dpick[...] = total.astype(BF)
        out(dpick, dpick_hbm)

    def leave(s):
        for copy in got[s, "core"]:
            copy.wait_recv()
        out(fin.at[:, :, :, rows(s)], fin_hbm.at[:, :, :, rows(s)])

    for stage, s in PLAN:
        dict(opp=opp, near=near, add=add, straight=straight, sum_y=sum_y, sum_z=sum_z, z_first=z_first,
             z_sum=z_sum, y_sum=y_sum, onto_x=onto_x, onto_core=onto_core, d_cores=d_cores,
             d_chips=d_chips, d_sum=d_sum, leave=leave)[stage](s)

    for copy in sends:
        copy.wait_send()
    for copy in outs:
        copy.wait()


def finish_kernel(fin_hbm, dpick_hbm, sel_hbm, d_tokens, gg, gu, gd,
                  fin, dpick, sel, rows, out_g, out_u, out_d, loaded, sems):
    loads = [pltpu.make_async_copy(sel_hbm, sel, loaded.at[4]),
             pltpu.make_async_copy(dpick_hbm, dpick, loaded.at[5])]
    parts = [pltpu.make_async_copy(fin_hbm.at[:, i], fin.at[:, i], loaded.at[i]) for i in range(4)]
    for copy in loads + [parts[i] for i in (3, 0, 1, 2)]:
        copy.start()
    copies = []

    def put(src, dst):
        copy = pltpu.make_async_copy(src, dst, sems.at[len(copies)])
        copy.start()
        copies.append(copy)

    for copy in loads:
        copy.wait()
    for k in range(4):
        at = pl.ds(k * 128, 128)
        rows[at] = dot(sel[:, at], dpick[...], ((0,), (0,))).astype(BF)
        put(rows.at[at], d_tokens.at[at])
    lane = iota((ROWS, 128), 1)
    parts[3].wait()
    rest = [fin[f, 3].astype(F32) for f in range(8)]
    for part, (out, dst) in enumerate(((out_g, gg), (out_u, gu), (out_d, gd))):
        parts[part].wait()
        for f in range(8):
            out[:, f * 128:(f + 1) * 128] = fin[f, part].astype(F32)
        for half in range(2):
            total = jnp.zeros((ROWS, 128), F32)
            for k in range(4):
                shift = ((k - part) * 32) % 128
                tile = rest[4 * half + k]
                tile = pltpu.roll(tile, shift, 1) if shift else tile
                total = jnp.where(lane // 32 == k, tile, total)
            out[:, 1024 + half * 128:1152 + half * 128] = total
        put(out, dst)
    for copy in copies:
        copy.wait()


def call(kernel, name, ins, outs, scratch=(), collective=None, flops=0):
    extra = {} if collective is None else dict(collective_id=collective, has_side_effects=True)
    vmem, any_ = pl.BlockSpec(memory_space=pltpu.VMEM), pl.BlockSpec(memory_space=pl.ANY)
    return pl.pallas_call(
        kernel,
        name=name,
        out_shape=[jax.ShapeDtypeStruct(shape, dtype) for shape, dtype, _ in outs],
        in_specs=[vmem if inside else any_ for inside in ins],
        out_specs=[vmem if inside else any_ for _, _, inside in outs],
        scratch_shapes=list(scratch),
        cost_estimate=pl.CostEstimate(flops=flops, bytes_accessed=8_000_000, transcendentals=0),
        compiler_params=pltpu.CompilerParams(vmem_limit_bytes=VMEM_LIMIT, **extra),
    )


def body(tokens, routes, gate_codes, cotangent, w_gate, w_up, w_down):
    dma = lambda n: pltpu.SemaphoreType.DMA((n,))
    buf = lambda *shape: pltpu.VMEM(shape, BF)
    quarter = buf(2, 2, ROWS, 128)
    half = buf(4, 2, ROWS, 128)
    fin, dpick, sel = call(
        expert_kernel, "expert", (1, 1, 0, 0, 0, 0, 0),
        [((4, 2, 4, ROWS, 128), BF, 0), ((CAP, D), BF, 0), ((CAP, TOK), BF, 0)],
        [buf(4, 2, 4, ROWS, 128), buf(CAP, D), buf(CAP, TOK), buf(TOK, D), buf(TOK, D), buf(3, ROWS, 128),
         buf(2, 8, CAP, D), buf(4, 8, ROWS, 128), pltpu.VMEM((4, D, 128), F32), buf(4, 2, 4, ROWS, 128),
         buf(8 * CAP, 384), buf(4, 2, CAP, D), buf(4, CAP, D), buf(3, CAP, D), buf(3, CAP, D),
         quarter, quarter, quarter, quarter, half, half, half, half, buf(7, ROWS, 128),
         buf(7, 4, ROWS, 128), buf(4, ROWS, 128), buf(3, ROWS, 128),
         dma(10 + NC), dma(19), dma(19), dma(14), dma(14), dma(13 * NC), dma(13 * NC), dma(4), dma(4),
         dma(19 * NC), dma(19 * NC),
         pltpu.SemaphoreType.REGULAR((3,))],
        collective=0, flops=4_000_000_000,
    )(routes.T, gate_codes.T, tokens, cotangent, w_gate, w_up, w_down)
    wide = pltpu.VMEM((ROWS, FF), F32)
    return tuple(call(
        finish_kernel, "finish", (0, 0, 0),
        [((TOK, D), BF, 0), ((ROWS, FF), F32, 0), ((ROWS, FF), F32, 0), ((ROWS, FF), F32, 0)],
        [buf(8, 4, ROWS, 128), buf(CAP, D), buf(CAP, TOK), buf(TOK, D), wide, wide, wide, dma(6), dma(7)], flops=200_000_000,
    )(fin.reshape(8, 4, ROWS, 128), dpick, sel))


def solution(mesh):
    both, dom = P(("rep", "dom"), None), P("dom", None)
    return jax.shard_map(
        body,
        mesh=mesh,
        in_specs=(both, both, both, both, dom, dom, dom),
        out_specs=(both, dom, dom, dom),
        check_vma=False,
    )
```

```python
import jax
import jax.numpy as jnp
from jax import lax
from jax.experimental import pallas as pl
from jax.experimental.pallas import tpu as pltpu
from jax.sharding import PartitionSpec as P

D, FF, CAP, TOK = 1792, 1280, 96, 512
ROWS = 224
HALF = CAP // 2
MESH = pl.DeviceIdType.MESH
BF, F32 = jnp.bfloat16, jnp.float32
VMEM_LIMIT = 56 * 1024 * 1024
CHUNKS = (
    (0, 48, "z", "steps"),
    (48, 80, "relay", "steps"),
    (128, 64, "relay", "steps"),
    (192, 32, "relay", "once"),
)
NC = len(CHUNKS)
PLAN = (
    ("z_first", 0), ("opp", 1), ("near", 1), ("opp", 2), ("d_cores", 0), ("add", 1), ("near", 2), ("opp", 3),
    ("d_chips", 0), ("add", 2), ("near", 3), ("sum_y", 1), ("add", 3), ("sum_y", 2), ("z_sum", 0),
    ("sum_y", 3), ("y_sum", 0), ("sum_z", 1), ("sum_z", 2), ("sum_z", 3), ("onto_x", 0), ("d_sum", 0),
    ("onto_x", 1), ("onto_x", 2), ("onto_core", 0), ("leave", 0), ("onto_x", 3), ("onto_core", 3),
    ("onto_core", 1), ("leave", 3), ("onto_core", 2), ("leave", 1), ("leave", 2),
)

POS = {0: 0, 1: 1, 3: 2, 2: 3}


def coords():
    r, d = lax.axis_index("rep"), lax.axis_index("dom")
    return r // 8, (r // 2) % 4, r % 2, d // 4, d % 4


def dev(x, zh, c, zl, y):
    return (x * 8 + zh * 2 + c, zl * 4 + y)


def dot(a, b, dims=((1,), (0,))):
    return lax.dot_general(a, b, (dims, ((), ())), preferred_element_type=F32)


def iota(shape, axis):
    return lax.broadcasted_iota(jnp.int32, shape, axis)


def swiglu_back(g, u, dh):
    sig = 1.0 / (1.0 + jnp.exp(-g))
    act = g * sig
    return dh * u * sig * (1.0 + g * (1.0 - sig)), dh * act, act * u


def rows_of(xa, kind, lo, hi):
    return xa[kind, lo:hi].reshape((hi - lo) * CAP, D)


def forward_picked(lo, hi, xa, wa):
    part = lambda i: wa[i].reshape(D, 128)
    picked = rows_of(xa, 0, lo, hi)
    return dot(picked, jnp.concatenate([part(0), part(1)], axis=1)), dot(picked, part(3))


def forward_scaled(lo, hi, xa, wa, pre, rest, back):
    n = (hi - lo) * CAP
    part = lambda i: wa[i].reshape(D, 128)
    down = dot(rows_of(xa, 1, lo, hi), jnp.concatenate([part(2), part(3)], axis=1))
    lane = iota((n, 128), 1)
    rest = jnp.where(lane < 64, rest, down[:, 128:])
    dg, du, hid = swiglu_back(pre[:, :128], pre[:, 128:], down[:, :128])
    dg_r, du_r, hid_r = swiglu_back(rest, pltpu.roll(rest, 96, 1), pltpu.roll(rest, 64, 1))
    mix = jnp.where(lane < 32, dg_r, pltpu.roll(du_r, 32, 1))
    rest_p = jnp.where(lane < 64, mix, 0.0).astype(BF)
    rest_s = jnp.where((lane >= 64) & (lane < 96), pltpu.roll(hid_r, 64, 1), 0.0).astype(BF)
    up = jnp.concatenate([dg, du], axis=1).astype(BF)
    low = jnp.concatenate([hid.astype(BF), rest_s], axis=1)
    back[lo * CAP:hi * CAP, :256] = up
    back[lo * CAP:hi * CAP, 256:] = rest_p
    return up, low, rest_p


def terms_of(lo, hi, xa, at, up, low, rest_p):
    n = (hi - lo) * CAP
    first = ((0,), (0,))
    p_k = xa[0, lo:hi, :, pl.ds(at, 256)].reshape(n, 256)
    s_k = xa[1, lo:hi, :, pl.ds(at, 256)].reshape(n, 256)
    gu, hr, rr = dot(p_k, up, first), dot(s_k, low, first), dot(p_k, rest_p, first)
    return gu[:, :128], gu[:, 128:], hr[:, :128], hr[:, 128:] + rr


def expert_kernel(
    routes, codes, tok_hbm, cot_hbm, wg, wu, wd, fin_hbm, dpick_hbm, sel_hbm,
    fin, dpick, sel_own, tok, cot, tail, xa, wa, grad, gb, back, dp, dr, ds, df, ra, rb, ta, tb, low, mid, high, zs, zr, zw, zy, yr,
    local, ts, tr, ws, wr, gs, gr, es, er, ns, nr, told,
):
    x, zh, c, zl, y = coords()
    z, f = zh * 2 + zl, 2 * x + c
    sib = dev(x, zh, 1 - c, zl, y)
    ring = [dev((x + k) % 4, zh, c, zl, y) for k in (1, 2, 3)]
    right, left = ring[0], ring[2]
    yn, ys = (y + 1) % 4, (y + 3) % 4
    north, south = dev(x, zh, c, zl, yn), dev(x, zh, c, zl, ys)
    column = [dev(x, ((z + k) % 8) // 2, c, ((z + k) % 8) % 2, y) for k in range(1, 8)]
    pair = dev(x, zh, c, 1 - zl, y)
    nearby = [right, left, north, south, column[0], column[6]]
    partners = [sib] + nearby

    barrier = pltpu.get_barrier_semaphore()
    for partner in partners:
        pl.semaphore_signal(barrier, inc=1, device_id=partner, device_id_type=MESH)

    dom, dom_z = zl * 4 + y, (1 - zl) * 4 + y
    tile = pl.multiple_of(f * 128, 128)
    last = pl.multiple_of(1024 + (f // 4) * 128, 128)
    loads = [
        pltpu.make_async_copy(tok_hbm, tok, local.at[0]),
        pltpu.make_async_copy(cot_hbm, cot, local.at[1]),
    ]
    for i, w in enumerate((wg, wu, wd)):
        loads.append(pltpu.make_async_copy(w.at[:, pl.ds(tile, 128)], wa.at[i, dom], local.at[2 + i]))
        loads.append(pltpu.make_async_copy(w.at[:, pl.ds(last, 128)], tail.at[i], local.at[5 + i]))
    for copy in loads:
        copy.start()

    sends, outs = [], []

    def out(src, dst):
        copy = pltpu.make_async_copy(src, dst, local.at[8 + len(outs)])
        copy.start()
        outs.append(copy)

    def send(sems, index, src, dst, device):
        copy = pltpu.make_async_remote_copy(
            src_ref=src, dst_ref=dst, send_sem=sems[0].at[index], recv_sem=sems[1].at[index],
            device_id=device, device_id_type=MESH,
        )
        copy.start()
        sends.append(copy)
        return copy

    T, W, G, E, N = (ts, tr), (ws, wr), (gs, gr), (es, er), (ns, nr)
    slot = lambda delta, other: 2 * POS[delta] + other

    member = routes[...] == 0
    routed = jnp.max(jnp.where(member, 1.0, 0.0), axis=0, keepdims=True)
    code = jnp.sum(jnp.where(member, codes[...], 0), axis=0, keepdims=True).astype(F32)
    before = jnp.where(iota((TOK, TOK), 0) < iota((TOK, TOK), 1), 1.0, 0.0).astype(BF)
    rank = dot(jnp.broadcast_to(routed, (16, TOK)).astype(BF), before)[:1]
    hit = (jnp.broadcast_to(rank, (CAP, TOK)) == iota((CAP, TOK), 0).astype(F32)) & (
        jnp.broadcast_to(routed, (CAP, TOK)) > 0.0)
    sel = jnp.where(hit, 1.0, 0.0)
    weight = jnp.sum(sel * code, axis=1, keepdims=True) * (1.0 / 256.0)
    sel = sel.astype(BF)
    sel_own[...] = sel
    out(sel_own, sel_hbm)
    loads[0].wait()
    xa[0, 0] = dot(sel, tok[...]).astype(BF)
    def weights(index, half, dom_y, device):
        block = wa.at[2 * half:2 * half + 2, dom_y]
        return send(W, index, block, block, device)

    def around(index, kind, lo, to_right):
        to, device = (slot(3, 0), right) if to_right else (slot(1, 0), left)
        return send(T, index, xa.at[kind, 0, lo:lo + HALF], xa.at[kind, to, lo:lo + HALF], device)

    def onward(index, kind, delta):
        lo, device = (0, right) if delta == 3 else (HALF, left)
        return send(T, index, xa.at[kind, slot(delta, 0), lo:lo + HALF],
                    xa.at[kind, slot(2, 0), lo:lo + HALF], device)

    def share(index, kind, delta):
        return send(T, index, xa.at[kind, slot(delta, 0)], xa.at[kind, slot(delta, 1)], sib)

    def tell(index, devices):
        for device in devices:
            pl.semaphore_signal(told.at[index], inc=1, device_id=device, device_id_type=MESH)

    here, there = zl * 4, (1 - zl) * 4
    pl.semaphore_wait(barrier, len(partners))
    p_right, p_left = around(0, 0, 0, True), around(1, 0, HALF, False)
    p_right_2, p_left_2 = around(15, 0, HALF, True), around(16, 0, 0, False)
    for copy in loads[2:]:
        copy.wait()
    rest = jnp.zeros((ROWS, 128), F32)
    src, dst = iota((128, 128), 0), iota((128, 128), 1)
    for part in range(3):
        move = (src - (f % 4) * 32 == dst - part * 32) & (dst // 32 == part)
        rest += dot(tail[part], jnp.where(move, 1.0, 0.0).astype(BF))
    wa[3, dom] = rest.astype(BF)
    north_0, south_1 = weights(0, 0, dom, north), weights(1, 1, dom, south)
    pair_0, pair_1 = weights(2, 0, dom, pair), weights(3, 1, dom, pair)
    north_1, south_0 = weights(4, 1, dom, north), weights(5, 0, dom, south)
    loads[1].wait()
    xa[1, 0] = (weight * dot(sel, cot[...])).astype(BF)
    s_right, s_left = around(2, 1, 0, True), around(3, 1, HALF, False)
    s_right_2, s_left_2 = around(17, 1, HALF, True), around(18, 1, 0, False)
    x_sib = send(T, 4, xa.at[:, 0], xa.at[:, slot(0, 1)], sib)

    tell(0, nearby)
    north_0.wait_recv()
    all_w = [weights(6, 0, here + ys, north)]
    south_1.wait_recv()
    all_w.append(weights(7, 1, here + yn, south))
    pair_0.wait_recv()
    z_north_0 = weights(8, 0, dom_z, north)
    pair_1.wait_recv()
    z_south_1 = weights(9, 1, dom_z, south)
    all_w += [weights(10, 1, dom_z, north), weights(11, 0, dom_z, south), north_1, south_0]
    pl.semaphore_wait(told.at[0], len(nearby))
    tell(1, (column[0], column[6]))
    p_right.wait_recv()
    p_on_r = onward(5, 0, 3)
    p_left.wait_recv()
    p_on_l = onward(6, 0, 1)
    p_right_2.wait_recv()
    p_left_2.wait_recv()
    share_p3, share_p1 = share(9, 0, 3), share(10, 0, 1)
    z_north_0.wait_recv()
    all_w.append(weights(12, 0, there + ys, north))
    z_south_1.wait_recv()
    all_w.append(weights(13, 1, there + yn, south))
    pl.semaphore_wait(told.at[1], 2)
    tell(2, (column[0], column[6]))
    s_right.wait_recv()
    s_on_r = onward(7, 1, 3)
    s_left.wait_recv()
    s_on_l = onward(8, 1, 1)
    s_right_2.wait_recv()
    s_left_2.wait_recv()
    share_s3, share_s1 = share(11, 1, 3), share(12, 1, 1)
    pl.semaphore_wait(told.at[2], 2)
    for copy in all_w + [x_sib, share_p3, share_p1, share_s3, share_s1]:
        copy.wait_recv()

    up6 = forward_scaled(0, 6, xa, wa, *forward_picked(0, 6, xa, wa), back)
    p_on_r.wait_recv()
    p_on_l.wait_recv()
    share_p2 = share(13, 0, 2)

    def columns(k, carry):
        at = pl.multiple_of(k * 256, 256)
        for i, term in enumerate(terms_of(0, 6, xa, at, *up6)):
            grad[i, pl.ds(at, 256), :] = term
        return carry

    lax.fori_loop(0, D // 256, columns, 0)
    s_on_r.wait_recv()
    s_on_l.wait_recv()
    share_s2 = share(14, 1, 2)
    share_p2.wait_recv()
    pre = forward_picked(6, 8, xa, wa)

    def token_part(lo, hi):
        for k in range(D // 256):
            flat = jnp.concatenate(
                [wa.at[i].reshape(D, 128)[k * 256:(k + 1) * 256] for i in (0, 1, 3)], axis=1)
            part = dot(back[2 * lo * CAP:2 * hi * CAP], flat, ((1,), (1,))).astype(BF)
            dp[lo:hi, :, :, k * 256:(k + 1) * 256] = part.reshape(hi - lo, 2, CAP, 256)

    token_part(0, 1)
    share_s2.wait_recv()
    up2 = forward_scaled(6, 8, xa, wa, *pre, back)
    for k in range(D // 256):
        lo = k * 256
        for i, term in enumerate(terms_of(6, 8, xa, lo, *up2)):
            total = (grad[i, lo:lo + 256, :] + term).astype(BF)
            at = lo
            while at < lo + 256:
                d, r = at // ROWS, at % ROWS
                n = min(ROWS - r, lo + 256 - at)
                gb[i, d // 4, d % 4, r:r + n, :] = total[at - lo:at - lo + n]
                at += n

    f32 = lambda ref: ref.astype(F32)
    opposite = (y + 2) % 4
    ways = [dev(x, zh, c, zl, (y + k) % 4) for k in (1, 2, 3)]
    got = {}

    def rows(s):
        return pl.ds(CHUNKS[s][0], CHUNKS[s][1])

    def opp(s):
        r = rows(s)
        got[s, "opp"] = (send(G, 13 * s, gb.at[0:2, :, opposite, r], ra.at[:, :, r], north),
                         send(G, 13 * s + 1, gb.at[2:4, :, opposite, r], rb.at[:, :, r], south))

    def near(s):
        r = rows(s)
        got[s, "y"] = [send(G, 13 * s + 2, gb.at[2:4, :, yn, r], low.at[2:4, :, r], north),
                       send(G, 13 * s + 3, gb.at[0:2, :, ys, r], high.at[0:2, :, r], south)]

    def add(s):
        r = rows(s)
        got[s, "opp"][0].wait_recv()
        ta[:, :, r] = (f32(ra[:, :, r]) + f32(gb[0:2, :, yn, r])).astype(BF)
        got[s, "y"].append(send(G, 13 * s + 4, ta.at[:, :, r], low.at[0:2, :, r], north))
        got[s, "opp"][1].wait_recv()
        tb[:, :, r] = (f32(rb[:, :, r]) + f32(gb[2:4, :, ys, r])).astype(BF)
        got[s, "y"].append(send(G, 13 * s + 5, tb.at[:, :, r], high.at[2:4, :, r], south))

    def straight(s):
        r = rows(s)
        got[s, "y"] = [send(G, 13 * s + k, gb.at[:, :, (y + k) % 4, r], to.at[:, :, r], ways[k - 1])
                       for k, to in ((2, mid), (1, low), (3, high))]

    def sum_y(s):
        r = rows(s)
        for copy in got[s, "y"]:
            copy.wait_recv()
        total = f32(gb[:, :, y, r]) + f32(low[:, :, r]) + f32(high[:, :, r])
        if CHUNKS[s][2] == "direct":
            total += f32(mid[:, :, r])
        zs[:, :, r] = total.astype(BF)
        got[s, "z"] = []
        for k in (4, 3, 5, 2, 6, 1, 7):
            to = (z + k) % 8
            got[s, "z"].append(send(G, 13 * s + 5 + k, zs.at[to // 2, to % 2, r], zr.at[k - 1, r],
                                    column[k - 1]))

    def sum_z(s):
        r = rows(s)
        for copy in got[s, "z"]:
            copy.wait_recv()
        total = f32(zs[zh, zl, r])
        for k in range(7):
            total += f32(zr[k, r])
        fin[x, c, zh, r] = total.astype(BF)
        spread(s)

    def z_first(s):
        r = rows(s)
        got[s, "z"] = []
        for k in (4, 3, 5, 2, 6, 1, 7):
            to = (z + k) % 8
            got[s, "z"].append(send(G, 13 * s + 5 + k, gb.at[to // 2, to % 2, :, r], zw.at[k - 1, :, r],
                                    column[k - 1]))

    def z_sum(s):
        r = rows(s)
        for copy in got[s, "z"]:
            copy.wait_recv()
        total = f32(gb[zh, zl, :, r])
        for k in range(7):
            total += f32(zw[k, :, r])
        zy[:, r] = total.astype(BF)
        got[s, "y"] = [send(G, 13 * s + k, zy.at[(y + k) % 4, r], yr.at[k - 1, r], ways[k - 1])
                       for k in (2, 1, 3)]

    def y_sum(s):
        r = rows(s)
        for copy in got[s, "y"]:
            copy.wait_recv()
        fin[x, c, zh, r] = (f32(zy[y, r]) + f32(yr[0, r]) + f32(yr[1, r]) + f32(yr[2, r])).astype(BF)
        spread(s)

    def spread(s):
        piece = fin.at[x, c, zh, rows(s)]
        if CHUNKS[s][3] == "steps":
            got[s, "zh"] = [send(N, 19 * s + k - 1, piece, piece, dev(x, (zh + k) % 4, c, zl, y))
                            for k in (1, 2, 3)]
            got[s, "x"] = {(j, 0): send(N, 19 * s + 2 + j, piece, piece, ring[j - 1]) for j in (2, 1, 3)}
        else:
            got[s, "x"] = {}
            for j, k in ((2, 2), (1, 2), (3, 2), (2, 1), (2, 3), (0, 2), (1, 1), (1, 3), (3, 1), (3, 3),
                         (2, 0), (0, 1), (0, 3), (1, 0), (3, 0)):
                got[s, "x"][j, k] = send(N, 19 * s + 4 * k + j - 1, piece, piece,
                                         dev((x + j) % 4, (zh + k) % 4, c, zl, y))

    def onto_x(s):
        if CHUNKS[s][3] == "steps":
            for k in (1, 3, 2):
                got[s, "zh"][k - 1].wait_recv()
                piece = fin.at[x, c, (zh + 4 - k) % 4, rows(s)]
                for j in (2, 1, 3):
                    got[s, "x"][j, k] = send(N, 19 * s + 2 + 3 * k + j, piece, piece, ring[j - 1])
        else:
            for k in (1, 3, 2):
                got[s, "x"][0, k].wait_recv()
        block = fin.at[x, c, :, rows(s)]
        got[s, "core"] = [send(N, 19 * s + 15, block, block, sib)]

    def onto_core(s):
        for j in (1, 3, 2):
            for k in range(4):
                got[s, "x"][j, k].wait_recv()
            block = fin.at[(x + 4 - j) % 4, c, :, rows(s)]
            got[s, "core"].append(send(N, 19 * s + 15 + j, block, block, sib))

    def d_cores(_):
        token_part(1, 4)
        got["d"] = send(E, 0, dp.at[:, 1], dr, sib)

    def d_chips(_):
        got["d"].wait_recv()
        for k in (2, 1, 3):
            ds[k - 1] = (f32(dr[POS[k]]) + f32(dp[POS[k], 0])).astype(BF)
            got["d", k] = send(E, k, ds.at[k - 1], df.at[k - 1], ring[k - 1])

    def d_sum(_):
        for k in (1, 2, 3):
            got["d", k].wait_recv()
        total = f32(dr[0]) + f32(dp[0, 0]) + f32(df[0]) + f32(df[1]) + f32(df[2])
        dpick[...] = total.astype(BF)
        out(dpick, dpick_hbm)

    def leave(s):
        for copy in got[s, "core"]:
            copy.wait_recv()
        out(fin.at[:, :, :, rows(s)], fin_hbm.at[:, :, :, rows(s)])

    for stage, s in PLAN:
        dict(opp=opp, near=near, add=add, straight=straight, sum_y=sum_y, sum_z=sum_z, z_first=z_first,
             z_sum=z_sum, y_sum=y_sum, onto_x=onto_x, onto_core=onto_core, d_cores=d_cores,
             d_chips=d_chips, d_sum=d_sum, leave=leave)[stage](s)

    for copy in sends:
        copy.wait_send()
    for copy in outs:
        copy.wait()


def finish_kernel(fin_hbm, dpick_hbm, sel_hbm, d_tokens, gg, gu, gd,
                  fin, dpick, sel, rows, out_g, out_u, out_d, loaded, sems):
    loads = [pltpu.make_async_copy(sel_hbm, sel, loaded.at[4]),
             pltpu.make_async_copy(dpick_hbm, dpick, loaded.at[5])]
    parts = [pltpu.make_async_copy(fin_hbm.at[:, i], fin.at[:, i], loaded.at[i]) for i in range(4)]
    for copy in loads + [parts[i] for i in (3, 0, 1, 2)]:
        copy.start()
    copies = []

    def put(src, dst):
        copy = pltpu.make_async_copy(src, dst, sems.at[len(copies)])
        copy.start()
        copies.append(copy)

    for copy in loads:
        copy.wait()
    for k in range(4):
        at = pl.ds(k * 128, 128)
        rows[at] = dot(sel[:, at], dpick[...], ((0,), (0,))).astype(BF)
        put(rows.at[at], d_tokens.at[at])
    lane = iota((ROWS, 128), 1)
    parts[3].wait()
    rest = [fin[f, 3].astype(F32) for f in range(8)]
    for part, (out, dst) in enumerate(((out_g, gg), (out_u, gu), (out_d, gd))):
        parts[part].wait()
        for f in range(8):
            out[:, f * 128:(f + 1) * 128] = fin[f, part].astype(F32)
        for half in range(2):
            total = jnp.zeros((ROWS, 128), F32)
            for k in range(4):
                shift = ((k - part) * 32) % 128
                tile = rest[4 * half + k]
                tile = pltpu.roll(tile, shift, 1) if shift else tile
                total = jnp.where(lane // 32 == k, tile, total)
            out[:, 1024 + half * 128:1152 + half * 128] = total
        put(out, dst)
    for copy in copies:
        copy.wait()


def call(kernel, name, ins, outs, scratch=(), collective=None, flops=0):
    extra = {} if collective is None else dict(collective_id=collective, has_side_effects=True)
    vmem, any_ = pl.BlockSpec(memory_space=pltpu.VMEM), pl.BlockSpec(memory_space=pl.ANY)
    return pl.pallas_call(
        kernel,
        name=name,
        out_shape=[jax.ShapeDtypeStruct(shape, dtype) for shape, dtype, _ in outs],
        in_specs=[vmem if inside else any_ for inside in ins],
        out_specs=[vmem if inside else any_ for _, _, inside in outs],
        scratch_shapes=list(scratch),
        cost_estimate=pl.CostEstimate(flops=flops, bytes_accessed=8_000_000, transcendentals=0),
        compiler_params=pltpu.CompilerParams(vmem_limit_bytes=VMEM_LIMIT, **extra),
    )


def body(tokens, routes, gate_codes, cotangent, w_gate, w_up, w_down):
    dma = lambda n: pltpu.SemaphoreType.DMA((n,))
    buf = lambda *shape: pltpu.VMEM(shape, BF)
    quarter = buf(2, 2, ROWS, 128)
    half = buf(4, 2, ROWS, 128)
    fin, dpick, sel = call(
        expert_kernel, "expert", (1, 1, 0, 0, 0, 0, 0),
        [((4, 2, 4, ROWS, 128), BF, 0), ((CAP, D), BF, 0), ((CAP, TOK), BF, 0)],
        [buf(4, 2, 4, ROWS, 128), buf(CAP, D), buf(CAP, TOK), buf(TOK, D), buf(TOK, D), buf(3, ROWS, 128),
         buf(2, 8, CAP, D), buf(4, 8, ROWS, 128), pltpu.VMEM((4, D, 128), F32), buf(4, 2, 4, ROWS, 128),
         buf(8 * CAP, 384), buf(4, 2, CAP, D), buf(4, CAP, D), buf(3, CAP, D), buf(3, CAP, D),
         quarter, quarter, quarter, quarter, half, half, half, half, buf(7, ROWS, 128),
         buf(7, 4, ROWS, 128), buf(4, ROWS, 128), buf(3, ROWS, 128),
         dma(10 + NC), dma(19), dma(19), dma(14), dma(14), dma(13 * NC), dma(13 * NC), dma(4), dma(4),
         dma(19 * NC), dma(19 * NC),
         pltpu.SemaphoreType.REGULAR((3,))],
        collective=0, flops=4_000_000_000,
    )(routes.T, gate_codes.T, tokens, cotangent, w_gate, w_up, w_down)
    wide = pltpu.VMEM((ROWS, FF), F32)
    return tuple(call(
        finish_kernel, "finish", (0, 0, 0),
        [((TOK, D), BF, 0), ((ROWS, FF), F32, 0), ((ROWS, FF), F32, 0), ((ROWS, FF), F32, 0)],
        [buf(8, 4, ROWS, 128), buf(CAP, D), buf(CAP, TOK), buf(TOK, D), wide, wide, wide, dma(6), dma(7)], flops=200_000_000,
    )(fin.reshape(8, 4, ROWS, 128), dpick, sel))


def solution(mesh):
    both, dom = P(("rep", "dom"), None), P("dom", None)
    return jax.shard_map(
        body,
        mesh=mesh,
        in_specs=(both, both, both, both, dom, dom, dom),
        out_specs=(both, dom, dom, dom),
        check_vma=False,
    )
```
